32 devices in a mesh: section: 2 (over y), wide: 4 (over z), narrow: 4 (over x, core).
Axes of the slice: x: 2, y: 2, z: 4, core: 2. Of those that a mesh axis runs over, the one named last changes fastest.
Arguments:
- token_shard: int32 [1024, 1], P(('section', 'wide')), may hold values from 0 to 7; in each aligned block of 128 rows (0 to 127, 128 to 255, ...) at most 32 rows name the same one
- token_row: int32 [1024], P(('section', 'wide')), may hold values from 0 to 511
- table: bfloat16 [4096, 8192], P(('section', 'wide'), 'narrow'), may hold values from -51 to 51
- gain: float32 [8192], P('narrow'), may hold values from 0.1 to 1.9
- key_value_weight: bfloat16 [2048, 8192], P(('section', 'wide'), 'narrow'), may hold values from -0.0625 to 0.0625
- kv_target: bfloat16 [1024, 2048], P(('section', 'wide'), 'narrow'), may hold values from -6 to 6
Outputs:
- table_grad: bfloat16 [4096, 8192], P(('section', 'wide'), 'narrow')
The draws below stay inside these ranges and needn't reach their ends.
Inputs may be any that keep to these rules, and one draw needn't show every extreme that they name: `token_shard`: among the rows of one device, no value is named by more than 32 rows.
All inputs are finite; a program needn't handle non-finite values.
Results may differ from the reference program's by a relative error of at most 0.0056.
Values may be sent and summed in bfloat16 or wider, within the bound.
No kernel may reach another device: no remote copies, remote signals or barrier semaphores. Data moves between devices by JAX's collectives and lax.ppermute only.
A program may use at most 64 MiB of HBM per device.

```python
import math
import jax
import jax.numpy as jnp
import numpy as np
from jax import lax

D = 8192
KV_WIDTH = 2048
VOCAB_DEV = 512
TOK_DEV = 128
OWNERS = 8
SLOTS = 32
VOCAB = 4096
TOKENS = 1024


def draw_table(key, part):
    row_key, jitter_key, base_key = jax.random.split(jax.random.fold_in(key, 11), 3)
    position = jnp.arange(D, dtype=jnp.float32)[None, :] / D
    jitter = jax.random.uniform(jitter_key, (1, D), jnp.float32, 0.7, 1.4)
    row_gain = jnp.exp(jax.random.uniform(row_key, (VOCAB, 1), jnp.float32, math.log(0.3), math.log(3.0)))
    column_gain = 0.3 * jnp.exp(math.log(10.0) * position) * jitter
    base = jnp.clip(jax.random.normal(base_key, (VOCAB, D), jnp.float32), -4.0, 4.0)
    return (base * row_gain * column_gain).astype(jnp.bfloat16)


def with_ends(entries, rng, low, largest):
    spot = [jax.random.randint(jax.random.fold_in(rng, axis), (), 0, length) for axis, length in enumerate(entries.shape)]
    widest = entries.shape.index(max(entries.shape))
    beside = spot[:widest] + [(spot[widest] + 1) % entries.shape[widest]] + spot[widest + 1:]
    return entries.at[tuple(spot)].set(low).at[tuple(beside)].set(largest)


def level_of(rng, extent, shards, least, largest):
    factor_of, own = 1.0, jax.random.fold_in(rng, 6)
    for axis_at, blocks in shards:
        steps = jnp.exp(jax.random.uniform(jax.random.fold_in(own, axis_at), (blocks,), jnp.float32, least / len(shards), largest / len(shards)))
        factor_of = factor_of * jnp.repeat(steps, extent[axis_at] // blocks).reshape([-1 if axis == axis_at else 1 for axis in range(len(extent))])
    return factor_of


def assign_block(stream_key, own, number, rows, amount, top, bound, lean):
    sequence = jax.random.permutation(stream_key, amount)
    heavy_load, usual = portions_of(amount, rows * top, bound, lean, True), portions_of(amount, rows * top, bound, lean, False)
    places = jnp.arange(amount)

    def named(sizes, offset_by):
        used = int((sizes > 0).sum())
        fixed = max(1, used // 4)
        shifted = fixed + (places - fixed + offset_by * (used - fixed)) % max(1, amount - fixed)
        return jnp.zeros((amount,), jnp.int32).at[sequence[jnp.where(places < fixed, places, shifted)]].set(jnp.asarray(sizes, jnp.int32))

    sizes = jnp.where(number % 4 == 0, named(heavy_load, number // 4), named(usual, number - number // 4 - 1))
    mixed = jax.random.permutation(jax.random.fold_in(own, 3), amount)
    donor, receiver = mixed[0:amount // 2 * 2:2], mixed[1:amount // 2 * 2:2]
    slack = jnp.minimum(sizes[donor] - 1, bound - sizes[receiver]) // 2
    slack = jnp.where((donor == sequence[0]) | (receiver == sequence[0]) | (sizes[receiver] == 0), 0, jnp.maximum(slack, 0))
    shifted = jax.random.randint(jax.random.fold_in(own, 4), (amount // 2,), 0, 1 << 20) % (slack + 1)
    sizes = sizes.at[donor].add(-shifted).at[receiver].add(shifted)
    items = jnp.searchsorted(jnp.cumsum(sizes), jnp.arange(rows * top), side="right").astype(jnp.int32)
    table = items.reshape(top, rows).T
    table = table[jax.random.permutation(jax.random.fold_in(own, 1), rows)]
    offset_by = jax.random.randint(jax.random.fold_in(own, 2), (rows, 1), 0, top)
    return jnp.take_along_axis(table, (jnp.arange(top)[None, :] + offset_by) % top, axis=1)


def portions_of(count, total, bound, skew, full):
    weights = [(1 << 20) // math.isqrt(standing ** skew) + 1 for standing in range(1, count + 1)]
    largest = bound if full else min(bound, max(-(-total // count), total * weights[0] // sum(weights)))
    least = 1 if total - largest >= count - 1 else 0
    counts, rest = [largest] + [least] * (count - 1), total - largest - least * (count - 1)
    while rest > 0:
        candidates = [i for i in range(1, count) if counts[i] < largest] or [i for i in range(1, count) if counts[i] < bound]
        mass, remaining = sum([weights[i] for i in candidates]), rest
        for i in candidates:
            more = min(bound - counts[i], max(1, remaining * weights[i] // mass), rest)
            counts[i] = counts[i] + more
            rest = rest - more
    return np.array(counts)


def normal_values(own_key, dims, width, reach, cuts=(), kind=jnp.bfloat16):
    result = width * jax.random.normal(own_key, dims, jnp.float32)
    if cuts:
        result = result * level_of(own_key, dims, cuts, -0.22, 0.18)
    return jnp.clip(result, -reach, reach).astype(kind)


def setup_inputs(seed: int = 0) -> dict:
    keys = jax.random.split(jax.random.key(seed), 7)
    token_shard_keys = jax.random.split(jax.random.fold_in(keys[0], 1), TOKENS // TOK_DEV)
    token_shard_turns = jax.random.permutation(jax.random.fold_in(keys[0], 3), TOKENS // TOK_DEV)
    token_shard = jax.vmap(lambda own, number: assign_block(jax.random.fold_in(keys[0], 2), own, number, TOK_DEV, OWNERS, 1, SLOTS, 1))(token_shard_keys, token_shard_turns).reshape((TOKENS, 1))
    token_row = with_ends(jax.random.randint(keys[1], (TOKENS,), 0, VOCAB_DEV), jax.random.fold_in(keys[1], 1), 0, VOCAB_DEV - 1).astype(jnp.int32)
    table = draw_table(jax.random.fold_in(keys[6], 71), 0)
    gain = jnp.clip(1.0 + 0.18 * jax.random.normal(keys[3], (D,), jnp.float32), 0.1, 1.9)
    key_value_weight = normal_values(keys[4], (KV_WIDTH, D), D ** -0.5, 0.0625, ((0, 8), (1, 4)))
    kv_target = normal_values(keys[5], (TOKENS, KV_WIDTH), 1.0, 6.0, ((0, 8), (1, 4)))
    return dict(token_shard=token_shard, token_row=token_row, table=table, gain=gain, key_value_weight=key_value_weight, kv_target=kv_target)


EPSILON = 1e-05

def reference(token_shard, token_row, table, gain, key_value_weight, kv_target):
    token_id = (token_shard[:, 0] * VOCAB_DEV + token_row).astype(jnp.int32)

    def block_pass(inputs):
        block_ids, block_target = inputs
        hidden = jnp.take(table, block_ids, axis=0)
        rows_float = hidden.astype(jnp.float32)
        mean_square = lax.optimization_barrier(jnp.sum(rows_float * rows_float, axis=1)) / D
        row_scale = lax.rsqrt(mean_square + EPSILON)
        normed = (rows_float * row_scale[:, None] * gain[None, :]).astype(jnp.bfloat16)
        projected = lax.dot_general(normed, key_value_weight, (((1,), (1,)), ((), ())), preferred_element_type=jnp.float32)
        residual = (projected - block_target.astype(jnp.float32)).astype(jnp.bfloat16)
        back_rows = jnp.dot(residual, key_value_weight, preferred_element_type=jnp.float32)
        weighted = back_rows * gain[None, :]
        inner_sum = lax.optimization_barrier(jnp.sum(weighted * rows_float, axis=1))
        grad_rows = row_scale[:, None] * weighted - rows_float * (row_scale ** 3 * inner_sum / D)[:, None]
        return grad_rows.astype(jnp.bfloat16)
    grouped = lax.map(block_pass, (token_id.reshape(-1, TOK_DEV), kv_target.reshape(-1, TOK_DEV, KV_WIDTH)))
    grad_rows = grouped.reshape(TOKENS, D)
    table_grad = jax.ops.segment_sum(grad_rows.astype(jnp.float32), token_id, num_segments=VOCAB)
    return table_grad.astype(jnp.bfloat16)
```

```python
import jax
import jax.numpy as jnp
from jax import lax
from jax.sharding import PartitionSpec as P

EPSILON = 1e-05

HOLDERS = ("section", "wide")
LANES = 128


def contract_last(left, right):
    return lax.dot_general(
        left, right, (((1,), (1,)), ((), ())), preferred_element_type=jnp.float32
    )


def contract_first(left, right):
    return lax.dot_general(
        left, right, (((0,), (0,)), ((), ())), preferred_element_type=jnp.float32
    )


def exchange_narrow(value, distance):
    narrow = lax.axis_size("narrow")
    return lax.ppermute(value, "narrow", [(i, i ^ distance) for i in range(narrow)])


def sum_narrow(value):
    distance = 1
    while distance < lax.axis_size("narrow"):
        value = value + exchange_narrow(value, distance)
        distance *= 2
    return value


def send_wide(value, pairs):
    return lax.ppermute(value, "wide", pairs)


def send_section(value):
    return lax.ppermute(value, "section", [(0, 1), (1, 0)])


def slots_of(shard_column, slot_count):
    tokens = shard_column.shape[0]
    shard_row = shard_column.reshape(1, tokens)
    earlier = lax.broadcasted_iota(jnp.int32, (tokens, tokens), 0) < lax.broadcasted_iota(
        jnp.int32, (tokens, tokens), 1
    )
    rank = jnp.sum(((shard_column == shard_row) & earlier).astype(jnp.int32), axis=0)
    position = shard_row * slot_count + rank[None, :]
    slots = lax.axis_size(HOLDERS) * slot_count
    return lax.broadcasted_iota(jnp.int32, (slots, tokens), 0) == position


def weight_pieces(weight):
    section, wide = lax.axis_index("section"), lax.axis_index("wide")
    rows = weight.shape[0]
    if lax.axis_size("section") != 2 or lax.axis_size("wide") != 4:
        whole = lax.all_gather(weight, HOLDERS, axis=0, tiled=True)
        size = 256
        return [
            (jnp.int32(at // size), whole[at : at + size])
            for at in range(0, whole.shape[0], size)
        ]
    half = rows // 2
    halves = (weight[:half], weight[half:])
    inner = (wide == 1) | (wide == 2)
    pair = [(0, 1), (1, 0), (2, 3), (3, 2)]
    middle = [(1, 2), (2, 1)]
    outward = [(1, 0), (2, 3)]
    here = section * 4
    there = (1 - section) * 4
    near, far = wide ^ 1, jnp.where(inner, 3 - wide, wide ^ 2)
    last = jnp.where(inner, wide ^ 2, 3 - wide)
    out = [(here + wide, 0, halves[0]), (here + wide, 1, halves[1])]
    p1 = [send_wide(w, pair) for w in halves]
    q2 = [send_wide(w, middle) for w in halves]
    y0 = [send_section(w) for w in halves]
    e1 = [send_wide(w, outward) for w in q2]
    q3 = [send_wide(w, middle) for w in p1]
    y1 = send_section(p1[0])
    e2 = [send_wide(w, outward) for w in q3]
    m2 = [jnp.where(inner, a, b) for a, b in zip(q2, e1)]
    y2 = [send_section(w) for w in m2]
    x1 = send_wide(y0[1], pair)
    m3 = [jnp.where(inner, a, b) for a, b in zip(q3, e2)]
    y3 = [send_section(w) for w in m3]
    out += [(there + wide, i, y0[i]) for i in range(2)]
    out += [(here + near, i, p1[i]) for i in range(2)]
    out += [(here + far, i, m2[i]) for i in range(2)]
    out += [(there + near, 0, y1)]
    out += [(there + far, i, y2[i]) for i in range(2)]
    out += [(here + last, i, m3[i]) for i in range(2)]
    out += [(there + near, 1, x1)]
    out += [(there + last, i, y3[i]) for i in range(2)]
    return [(holder * 2 + part, piece) for holder, part, piece in out]


def on_device(token_shard, token_row, table, gain, key_value_weight, kv_target):
    tokens_here = token_row.shape[0]
    owners = lax.axis_size(HOLDERS)
    narrow = lax.axis_size("narrow")
    slot_count = 2 * tokens_here // owners
    slots = owners * slot_count
    vocab_rows, width_here = table.shape
    width = width_here * narrow
    target_width = kv_target.shape[1]
    pieces = weight_pieces(key_value_weight)

    to_slot = slots_of(token_shard, slot_count).astype(jnp.bfloat16)
    row_parts = jnp.stack(
        [token_row // 256, token_row % 256, jnp.ones_like(token_row)], axis=1
    ).astype(jnp.bfloat16)
    row_parts = jnp.pad(row_parts, ((0, 0), (0, LANES - 3)))
    sent = jnp.dot(
        to_slot,
        jnp.concatenate([kv_target, row_parts], axis=1),
        preferred_element_type=jnp.float32,
    ).astype(jnp.bfloat16)
    arrived = lax.all_to_all(
        sent.reshape(owners, slot_count, target_width + LANES),
        HOLDERS,
        split_axis=0,
        concat_axis=0,
        tiled=True,
    ).reshape(slots, target_width + LANES)
    row_parts = arrived[:, target_width : target_width + 3].astype(jnp.float32)
    row = (row_parts[:, :1] * 256 + row_parts[:, 1:2]).astype(jnp.int32)
    row = jnp.where(row_parts[:, 2:3] > 0.5, row, -1)
    picks = (row == lax.broadcasted_iota(jnp.int32, (slots, vocab_rows), 1)).astype(jnp.bfloat16)
    hidden = jnp.dot(picks, table, preferred_element_type=jnp.float32).astype(jnp.bfloat16)
    rows_float = hidden.astype(jnp.float32)
    mean_square = sum_narrow(jnp.sum(rows_float * rows_float, axis=1, keepdims=True)) / width
    row_scale = lax.rsqrt(mean_square + EPSILON)
    normed = (rows_float * row_scale * gain[None, :]).astype(jnp.bfloat16)

    target_here = arrived[:, :target_width]
    targets = jnp.stack(
        [target_here] + [exchange_narrow(target_here, d) for d in range(1, narrow)]
    )
    my_narrow = lax.axis_index("narrow")

    back_rows = jnp.zeros((slots, width_here), jnp.float32)
    inner_sum = jnp.zeros((slots, 1), jnp.float32)
    for place, piece in pieces:
        features = piece.shape[0]
        at = place * features
        projected = sum_narrow(contract_last(normed, piece))
        source = at // target_width
        target = lax.dynamic_slice(
            targets, (source ^ my_narrow, 0, at % target_width), (1, slots, features)
        )[0]
        residual = (projected - target.astype(jnp.float32)).astype(jnp.bfloat16)
        inner_sum += jnp.sum(residual.astype(jnp.float32) * projected, axis=1, keepdims=True)
        back_rows += jnp.dot(residual, piece, preferred_element_type=jnp.float32)

    grad_rows = (
        row_scale * (back_rows * gain[None, :])
        - rows_float * (row_scale * row_scale * inner_sum / width)
    ).astype(jnp.bfloat16)
    return contract_first(picks, grad_rows).astype(jnp.bfloat16)


def solution(mesh):
    return jax.shard_map(
        on_device,
        mesh=mesh,
        in_specs=(
            P(("section", "wide"), None),
            P(("section", "wide")),
            P(("section", "wide"), "narrow"),
            P("narrow"),
            P(("section", "wide"), "narrow"),
            P(("section", "wide"), "narrow"),
        ),
        out_specs=P(("section", "wide"), "narrow"),
        check_vma=False,
    )
```

```python
import functools

import jax
import jax.numpy as jnp
from jax import lax
from jax.experimental import pallas as pl
from jax.experimental.pallas import tpu as pltpu
from jax.sharding import PartitionSpec as P

EPSILON = 1e-05

HOLDERS = ("section", "wide")
LANES = 128
COLUMNS = 512
SMALL_COST = pl.CostEstimate(flops=1000, bytes_accessed=1000, transcendentals=0)


def contract_last(left, right):
    return lax.dot_general(
        left, right, (((1,), (1,)), ((), ())), preferred_element_type=jnp.float32
    )


def dot(left, right):
    return jnp.dot(left, right, preferred_element_type=jnp.float32)


def local_kernel(body, out_shape, mebibytes=8, **kwargs):
    return pl.pallas_call(
        body,
        out_shape=out_shape,
        compiler_params=pltpu.CompilerParams(vmem_limit_bytes=mebibytes * 1024 * 1024),
        cost_estimate=SMALL_COST,
        **kwargs,
    )


def anywhere(count):
    return [pl.BlockSpec(memory_space=pl.ANY)] * count


def gate(values, after):
    count = len(values)
    return pl.pallas_call(
        lambda *refs: None,
        out_shape=[jax.ShapeDtypeStruct(v.shape, v.dtype) for v in values],
        in_specs=anywhere(count + len(after)),
        out_specs=anywhere(count),
        input_output_aliases={i: i for i in range(count)},
        cost_estimate=SMALL_COST,
    )(*values, *after)


def in_vmem(count):
    return [pl.BlockSpec(memory_space=pltpu.VMEM)] * count


def slots_body(slot_count, shard_row, token_row, target, _, sent):
    tokens, width = target.shape
    slots = sent.shape[0]
    shard_here = shard_row[...]
    earlier = lax.broadcasted_iota(jnp.int32, (tokens, tokens), 0) < lax.broadcasted_iota(
        jnp.int32, (tokens, tokens), 1
    )
    shard_column = jnp.broadcast_to(shard_here.astype(jnp.float32), (tokens, tokens)).T
    same = (shard_column.astype(jnp.int32) == shard_here) & earlier
    rank = jnp.sum(jnp.where(same, 1.0, 0.0), axis=0, keepdims=True).astype(jnp.int32)
    position = shard_here * slot_count + rank
    here = lax.broadcasted_iota(jnp.int32, (slots, tokens), 0) == position
    to_slot = jnp.where(here, 1.0, 0.0)
    sent[:, :width] = dot(to_slot.astype(jnp.bfloat16), target[...]).astype(jnp.bfloat16)
    row = token_row[...]
    high = jnp.sum(to_slot * (row >> 8).astype(jnp.float32), axis=1, keepdims=True)
    low = jnp.sum(to_slot * (row & 255).astype(jnp.float32), axis=1, keepdims=True)
    taken = jnp.sum(to_slot, axis=1, keepdims=True)
    lane = lax.broadcasted_iota(jnp.int32, (slots, LANES), 1)
    numbers = jnp.where(
        lane == 0, high, jnp.where(lane == 1, low, jnp.where(lane == 2, taken, 0.0))
    )
    sent[:, width:] = numbers.astype(jnp.bfloat16)


def pick_body(arrived, table, hidden, squares, target, place, rows_buffer, copied):
    vocab_rows, width = table.shape
    target_width = target.shape[0] * LANES
    parts = [slice(at, at + COLUMNS) for at in range(0, width, COLUMNS)]
    copies = [
        pltpu.make_async_copy(table.at[:, part], rows_buffer.at[:, part], copied.at[i])
        for i, part in enumerate(parts)
    ]
    for copy in copies:
        copy.start()
    here = arrived[...]
    slots = here.shape[0]
    numbers = here[:, target_width:].astype(jnp.float32)
    row = jnp.where(numbers[:, 2:3] > 0.5, numbers[:, 0:1] * 256.0 + numbers[:, 1:2], -1.0)
    picks = jnp.where(
        row.astype(jnp.int32) == lax.broadcasted_iota(jnp.int32, (slots, vocab_rows), 1), 1.0, 0.0
    )
    place[...] = picks.T.astype(jnp.bfloat16)
    picks = picks.astype(jnp.bfloat16)
    for i in range(target.shape[0]):
        target[i] = here[:, i * LANES : (i + 1) * LANES]
    total = jnp.zeros((slots, LANES), jnp.float32)
    for copy, part in zip(copies, parts):
        copy.wait()
        rows = dot(picks, rows_buffer[:, part])
        hidden[:, part] = rows.astype(jnp.bfloat16)
        for lane in range(0, COLUMNS, LANES):
            value = rows[:, lane : lane + LANES]
            total += value * value
    squares[...] = total


def norm_body(width, hidden, gain, squares, others, normed, scale):
    mean_square = jnp.sum(squares[...] + others[...], axis=1, keepdims=True) / width
    row_scale = lax.rsqrt(mean_square + EPSILON)
    scale[...] = jnp.broadcast_to(row_scale, scale.shape)
    for at in range(0, hidden.shape[1], COLUMNS):
        columns = slice(at, at + COLUMNS)
        rows = hidden[:, columns].astype(jnp.float32)
        normed[:, columns] = (rows * row_scale * gain[:, columns]).astype(jnp.bfloat16)


def start_pieces(pieces, buffer, copied):
    copies = []
    for i, piece in enumerate(pieces):
        there = buffer.at[pl.ds(i * LANES, LANES)]
        copies.append(pltpu.make_async_copy(piece, there, copied.at[i]))
        copies[-1].start()
    return copies


def forward_body(count, normed, *refs):
    pieces, (out, rows_buffer, buffer, copied) = refs[:count], refs[count:]
    rows = pltpu.make_async_copy(normed, rows_buffer, copied.at[count])
    rows.start()
    copies = start_pieces(pieces, buffer, copied)
    rows.wait()
    for i in range(0, count, 2):
        for copy in copies[i : i + 2]:
            copy.wait()
        part = slice(i * LANES, min(i + 2, count) * LANES)
        out[:, part] = contract_last(rows_buffer[...], buffer[part])


def target_at(places, i, targets):
    distance, block = places[0, i], places[1, i]
    value = targets[0][block].astype(jnp.float32)
    for d in range(1, len(targets)):
        value = jnp.where(distance == d, targets[d][block].astype(jnp.float32), value)
    return value


def residual_of(places, first, projected, others, targets, inner, residual):
    for i in range(projected.shape[1] // LANES):
        lanes = slice(i * LANES, (i + 1) * LANES)
        value = projected[:, lanes].astype(jnp.float32) + others[:, lanes].astype(jnp.float32)
        rounded = (value - target_at(places, first + i, targets)).astype(jnp.bfloat16)
        residual[:, (first + i) * LANES : (first + i + 1) * LANES] = rounded
        inner = inner + rounded.astype(jnp.float32) * value
    return inner


def residuals_of(places, summed, targets, inner, residual):
    first = 0
    for projected, others in zip(summed[::2], summed[1::2]):
        inner = residual_of(places, first, projected, others, targets, inner, residual)
        first += projected.shape[1] // LANES
    return inner


def back_body(count, sums, narrow, before, places, *refs):
    pieces, refs = refs[:count], refs[count:]
    summed, refs = refs[: 2 * sums], refs[2 * sums :]
    targets, refs = refs[:narrow], refs[narrow:]
    if before:
        back_in, inner_in, refs = refs[0], refs[1], refs[2:]
    back_out, inner_out, residual, buffer, copied = refs
    copies = start_pieces(pieces, buffer, copied)
    inner = inner_in[...] if before else jnp.zeros(inner_out.shape, jnp.float32)
    inner_out[...] = residuals_of(places, summed, targets, inner, residual)
    for copy in copies:
        copy.wait()
    for at in range(0, back_out.shape[1], COLUMNS):
        part = slice(at, at + COLUMNS)
        value = dot(residual[...], buffer[:, part])
        back_out[:, part] = value + back_in[:, part] if before else value


def tail_body(count, sums, narrow, width, places, *refs):
    pieces, refs = refs[:count], refs[count:]
    summed, refs = refs[: 2 * sums], refs[2 * sums :]
    targets, refs = refs[:narrow], refs[narrow:]
    back_in, inner_in, hidden, gain, scale, place, table_grad, residual, factor = refs

    @pl.when(pl.program_id(0) == 0)
    def _():
        inner = residuals_of(places, summed, targets, inner_in[...], residual)
        inner = jnp.sum(inner, axis=1, keepdims=True)
        factor[...] = scale[...] * scale[...] * (inner / width)

    back = back_in[...]
    for i, piece in enumerate(pieces):
        back += dot(residual[:, i * LANES : (i + 1) * LANES], piece[...])
    row_grad = scale[:, :1] * (back * gain[...]) - hidden[...].astype(jnp.float32) * factor[:, :1]
    table_grad[...] = dot(place[...], row_grad.astype(jnp.bfloat16)).astype(jnp.bfloat16)


def whole_block(shape):
    return pl.BlockSpec(shape, lambda i, *_: (0,) * len(shape))


def column_block(rows):
    return pl.BlockSpec((rows, COLUMNS), lambda i, *_: (0, i))


def exchange_narrow(value, distance):
    narrow = lax.axis_size("narrow")
    return lax.ppermute(value, "narrow", [(i, i ^ distance) for i in range(narrow)])


class Device:
    def __init__(self, token_shard, token_row, table, gain, kv_target):
        self.tokens = (token_shard, token_row, kv_target)
        self.table = table
        self.gain = gain.reshape(1, table.shape[1])
        self.owners = lax.axis_size(HOLDERS)
        self.slot_count = 2 * kv_target.shape[0] // self.owners
        self.slots = self.owners * self.slot_count
        self.blocks = kv_target.shape[1] // LANES
        self.width_all = table.shape[1] * lax.axis_size("narrow")
        self.before = ()

    def ask(self, after):
        token_shard, token_row, target = self.tokens
        tokens, width = target.shape
        sent = local_kernel(
            functools.partial(slots_body, self.slot_count),
            jax.ShapeDtypeStruct((self.slots, width + LANES), jnp.bfloat16),
            in_specs=in_vmem(3) + anywhere(1),
        )(token_shard.reshape(1, tokens), token_row.reshape(1, tokens), target, after)
        self.arrived = lax.all_to_all(
            sent.reshape(self.owners, self.slot_count, width + LANES),
            HOLDERS,
            split_axis=0,
            concat_axis=0,
            tiled=True,
        ).reshape(self.slots, width + LANES)
        return self.arrived

    def pick(self):
        vocab_rows, width = self.table.shape
        self.hidden, squares, self.target, self.place = local_kernel(
            pick_body,
            (
                jax.ShapeDtypeStruct((self.slots, width), jnp.bfloat16),
                jax.ShapeDtypeStruct((self.slots, LANES), jnp.float32),
                jax.ShapeDtypeStruct((self.blocks, self.slots, LANES), jnp.bfloat16),
                jax.ShapeDtypeStruct((vocab_rows, self.slots), jnp.bfloat16),
            ),
            mebibytes=12,
            in_specs=in_vmem(1) + anywhere(1),
            scratch_shapes=[
                pltpu.VMEM((vocab_rows, width), jnp.bfloat16),
                pltpu.SemaphoreType.DMA((width // COLUMNS,)),
            ],
        )(self.arrived, self.table)
        return squares

    def norm(self, squares, others):
        self.normed, self.scale = local_kernel(
            functools.partial(norm_body, self.width_all),
            (
                jax.ShapeDtypeStruct(self.hidden.shape, jnp.bfloat16),
                jax.ShapeDtypeStruct((self.slots, LANES), jnp.float32),
            ),
        )(self.hidden, self.gain, squares, others)

    def share_targets(self):
        others = [exchange_narrow(self.target, d) for d in range(1, lax.axis_size("narrow"))]
        self.targets = [self.target] + others

    def forward(self, group):
        count = len(group)
        slots, width = self.normed.shape
        return local_kernel(
            functools.partial(forward_body, count),
            jax.ShapeDtypeStruct((slots, count * LANES), jnp.float32),
            in_specs=anywhere(1 + count),
            scratch_shapes=[
                pltpu.VMEM((slots, width), jnp.bfloat16),
                pltpu.VMEM((count * LANES, width), jnp.bfloat16),
                pltpu.SemaphoreType.DMA((count + 1,)),
            ],
        )(self.normed, *[piece for _, piece in group])

    def places(self, group):
        at = jnp.stack([which for which, _ in group])
        distance = (at // self.blocks) ^ lax.axis_index("narrow")
        return jnp.stack([distance, at % self.blocks])

    def back(self, group, *summed):
        slots, width = self.normed.shape
        count, narrow = len(group), len(self.targets)
        self.before = local_kernel(
            functools.partial(back_body, count, len(summed) // 2, narrow, len(self.before) > 0),
            (
                jax.ShapeDtypeStruct((slots, width), jnp.float32),
                jax.ShapeDtypeStruct((slots, LANES), jnp.float32),
            ),
            mebibytes=16,
            in_specs=[pl.BlockSpec(memory_space=pltpu.SMEM)]
            + anywhere(count)
            + in_vmem(len(summed) + narrow + len(self.before)),
            scratch_shapes=[
                pltpu.VMEM((slots, count * LANES), jnp.bfloat16),
                pltpu.VMEM((count * LANES, width), jnp.bfloat16),
                pltpu.SemaphoreType.DMA((count,)),
            ],
        )(
            self.places(group),
            *[piece for _, piece in group],
            *summed,
            *self.targets,
            *self.before,
        )
        return self.before[1]

    def tail(self, group, *summed):
        slots, width = self.normed.shape
        vocab_rows = self.place.shape[0]
        count, narrow = len(group), len(self.targets)
        lanes = whole_block((slots, LANES))
        return local_kernel(
            functools.partial(tail_body, count, len(summed) // 2, narrow, self.width_all),
            jax.ShapeDtypeStruct((vocab_rows, width), jnp.bfloat16),
            mebibytes=16,
            grid_spec=pltpu.PrefetchScalarGridSpec(
                num_scalar_prefetch=1,
                grid=(width // COLUMNS,),
                in_specs=[column_block(LANES)] * count
                + [whole_block(value.shape) for value in summed]
                + [whole_block(self.target.shape)] * narrow
                + [column_block(slots), lanes, column_block(slots), column_block(1), lanes]
                + [whole_block(self.place.shape)],
                out_specs=column_block(vocab_rows),
                scratch_shapes=[
                    pltpu.VMEM((slots, count * LANES), jnp.bfloat16),
                    pltpu.VMEM((slots, LANES), jnp.float32),
                ],
            ),
        )(
            self.places(group),
            *[piece for _, piece in group],
            *summed,
            *self.targets,
            *self.before,
            self.hidden,
            self.gain,
            self.scale,
            self.place,
        )


SUM_TYPE = jnp.bfloat16


def sum_of_cores(value):
    return (value + exchange_narrow(value, 1)).astype(SUM_TYPE)


def plain_order(device, weight):
    device.ask(weight)
    squares = device.pick()
    squares += exchange_narrow(squares, 1)
    device.norm(squares, exchange_narrow(squares, 2))
    device.share_targets()
    whole = lax.all_gather(weight, HOLDERS, axis=0, tiled=True)
    pieces = [
        (jnp.int32(at // LANES), whole[at : at + LANES]) for at in range(0, whole.shape[0], LANES)
    ]
    groups = [pieces[i : i + 4] for i in range(0, len(pieces), 4)]
    for number, group in enumerate(groups):
        half = sum_of_cores(device.forward(group))
        step = device.back if number < len(groups) - 1 else device.tail
        result = step(group, half, exchange_narrow(half, 2))
    return result


def ring_order(device, weight):
    section, wide = lax.axis_index("section"), lax.axis_index("wide")
    holders = lax.axis_size(HOLDERS)
    at_ring = [i if i < holders // 2 else holders + holders // 2 - 1 - i for i in range(holders)]
    ring = jnp.where(section == 0, wide, holders - 1 - wide)

    def send(value, step):
        pairs = [(at_ring[i], at_ring[(i + step) % holders]) for i in range(holders)]
        return lax.ppermute(value, HOLDERS, pairs)

    def named(distance, half, piece):
        at = (ring + distance) % holders
        holder = jnp.where(at < holders // 2, at, holders + holders // 2 - 1 - at)
        return 2 * holder + half, piece

    w0, w1 = weight[:LANES], weight[LANES:]
    own = [named(0, 0, w0), named(0, 1, w1)]
    up0, down1 = send(w0, 1), send(w1, -1)
    up1, down0 = send(w1, 1), send(w0, -1)

    up0, down1 = gate([up0, down1], [])
    near = [named(-1, 0, up0), named(1, 1, down1)]
    up0, down1 = send(up0, 1), send(down1, -1)
    device.ask(near[0][1])

    up1, down0 = gate([up1, down0], [])
    near += [named(-1, 1, up1), named(1, 0, down0)]
    up1, down0 = send(up1, 1), send(down0, -1)
    squares = device.pick()
    squares += exchange_narrow(squares, 1)
    squares_other = exchange_narrow(squares, 2)

    up0, down1 = gate([up0, down1], [squares])
    second = [named(-2, 0, up0), named(2, 1, down1)]
    up0, down1 = send(up0, 1), send(down1, -1)
    device.norm(squares, squares_other)
    group0 = own + near
    sum0 = device.forward(group0)
    device.share_targets()

    up1, down0 = gate([up1, down0], [sum0])
    second += [named(-2, 1, up1), named(2, 0, down0)]
    up1, down0 = send(up1, 1), send(down0, -1)
    half0 = sum_of_cores(sum0)
    other0 = exchange_narrow(half0, 2)
    sum1 = device.forward(second)

    up0, down1 = gate([up0, down1], [sum1, half0])
    third = [named(-3, 0, up0), named(3, 1, down1)]
    up0, down1 = send(up0, 1), send(down1, -1)
    half1 = sum_of_cores(sum1)
    other1 = exchange_narrow(half1, 2)

    up1, down0 = gate([up1, down0], [half1])
    third += [named(-3, 1, up1), named(3, 0, down0)]
    sum2 = device.forward(third)
    half2 = sum_of_cores(sum2)
    other2 = exchange_narrow(half2, 2)
    done = device.back(group0 + second, half0, other0, half1, other1)

    up0, down1 = gate([up0, down1], [done, half2])
    last = [named(4, 0, up0), named(4, 1, down1)]
    half3 = sum_of_cores(device.forward(last))
    return device.tail(third + last, half2, other2, half3, exchange_narrow(half3, 2))


def on_device(token_shard, token_row, table, gain, key_value_weight, kv_target):
    device = Device(token_shard, token_row, table, gain, kv_target)
    holders = (lax.axis_size("section"), lax.axis_size("wide"))
    if holders == (2, 4) and key_value_weight.shape[0] == 2 * LANES:
        return ring_order(device, key_value_weight)
    return plain_order(device, key_value_weight)


def solution(mesh):
    return jax.shard_map(
        on_device,
        mesh=mesh,
        in_specs=(
            P(("section", "wide"), None),
            P(("section", "wide")),
            P(("section", "wide"), "narrow"),
            P("narrow"),
            P(("section", "wide"), "narrow"),
            P(("section", "wide"), "narrow"),
        ),
        out_specs=P(("section", "wide"), "narrow"),
        check_vma=False,
    )
```

```python
import functools

import jax
import jax.numpy as jnp
from jax import lax
from jax.experimental import pallas as pl
from jax.experimental.pallas import tpu as pltpu
from jax.sharding import PartitionSpec as P

EPSILON = 1e-05

HOLDERS = ("section", "wide")
LANES = 128
COLUMNS = 512
SMALL_COST = pl.CostEstimate(flops=1000, bytes_accessed=1000, transcendentals=0)


def contract_last(left, right):
    return lax.dot_general(
        left, right, (((1,), (1,)), ((), ())), preferred_element_type=jnp.float32
    )


def dot(left, right):
    return jnp.dot(left, right, preferred_element_type=jnp.float32)


VMEM_BYTES = 63 * 1024 * 1024


def local_kernel(body, out_shape, **kwargs):
    return pl.pallas_call(
        body,
        out_shape=out_shape,
        compiler_params=pltpu.CompilerParams(vmem_limit_bytes=VMEM_BYTES),
        cost_estimate=SMALL_COST,
        **kwargs,
    )


def in_hbm(count):
    return [pl.BlockSpec(memory_space=pltpu.HBM)] * count


TOKEN = jax.ShapeDtypeStruct((8, LANES), jnp.float32)


def gate(values, *after):
    count = len(values)
    *values, token = local_kernel(
        lambda *refs: None,
        [jax.ShapeDtypeStruct(v.shape, v.dtype) for v in values] + [TOKEN],
        in_specs=in_hbm(count + len(after)),
        out_specs=in_hbm(count + 1),
        input_output_aliases={i: i for i in range(count)},
    )(*values, *after)
    return values, token


def halves_body(up, down, *refs):
    up_half, down_half, _, buffer, copied = refs[-5:]
    rows = up_half.shape[0]
    ends = [(up.at[pl.ds(0, rows)], up_half), (down.at[pl.ds(rows, rows)], down_half)]
    copies = [
        [
            pltpu.make_async_copy(source, buffer.at[i], copied.at[2 * i]),
            pltpu.make_async_copy(buffer.at[i], result, copied.at[2 * i + 1]),
        ]
        for i, (source, result) in enumerate(ends)
    ]
    for first, _ in copies:
        first.start()
    for first, second in copies:
        first.wait()
        second.start()
    for _, second in copies:
        second.wait()


def gate_halves(up, down, *after):
    half = jax.ShapeDtypeStruct((up.shape[0] // 2, up.shape[1]), up.dtype)
    return local_kernel(
        halves_body,
        [half, half, TOKEN],
        in_specs=in_hbm(2 + len(after)),
        out_specs=in_hbm(3),
        scratch_shapes=[
            pltpu.VMEM((2, *half.shape), half.dtype),
            pltpu.SemaphoreType.DMA((4,)),
        ],
    )(up, down, *after)


def in_vmem(count):
    return [pl.BlockSpec(memory_space=pltpu.VMEM)] * count


def slots_body(slot_count, shard_row, token_row, target, sent):
    tokens, width = target.shape
    slots = sent.shape[0]
    shard_here = shard_row[...]
    earlier = lax.broadcasted_iota(jnp.int32, (tokens, tokens), 0) < lax.broadcasted_iota(
        jnp.int32, (tokens, tokens), 1
    )
    shard_column = jnp.broadcast_to(shard_here.astype(jnp.float32), (tokens, tokens)).T
    same = (shard_column.astype(jnp.int32) == shard_here) & earlier
    rank = jnp.sum(jnp.where(same, 1.0, 0.0), axis=0, keepdims=True).astype(jnp.int32)
    position = shard_here * slot_count + rank
    here = lax.broadcasted_iota(jnp.int32, (slots, tokens), 0) == position
    to_slot = jnp.where(here, 1.0, 0.0)
    sent[:, :width] = dot(to_slot.astype(jnp.bfloat16), target[...]).astype(jnp.bfloat16)
    row = token_row[...]
    high = jnp.sum(to_slot * (row >> 8).astype(jnp.float32), axis=1, keepdims=True)
    low = jnp.sum(to_slot * (row & 255).astype(jnp.float32), axis=1, keepdims=True)
    taken = jnp.sum(to_slot, axis=1, keepdims=True)
    lane = lax.broadcasted_iota(jnp.int32, (slots, LANES), 1)
    numbers = jnp.where(
        lane == 0, high, jnp.where(lane == 1, low, jnp.where(lane == 2, taken, 0.0))
    )
    sent[:, width:] = numbers.astype(jnp.bfloat16)


def pick_body(arrived, table, gain, _, hidden, scaled, squares, target, place, rows_buffer, copied):
    vocab_rows, width = table.shape
    target_width = target.shape[0] * LANES
    blocks = [slice(at, at + COLUMNS) for at in range(0, width, COLUMNS)]
    copies = [
        pltpu.make_async_copy(table.at[:, block], rows_buffer.at[:, block], copied.at[i])
        for i, block in enumerate(blocks)
    ]
    for copy in copies:
        copy.start()
    here = arrived[...]
    slots = here.shape[0]
    numbers = here[:, target_width:].astype(jnp.float32)
    row = jnp.where(numbers[:, 2:3] > 0.5, numbers[:, 0:1] * 256.0 + numbers[:, 1:2], -1.0)
    picks = jnp.where(
        row.astype(jnp.int32) == lax.broadcasted_iota(jnp.int32, (slots, vocab_rows), 1), 1.0, 0.0
    )
    place[...] = picks.T.astype(jnp.bfloat16)
    picks = picks.astype(jnp.bfloat16)
    for i in range(target.shape[0]):
        target[i] = here[:, i * LANES : (i + 1) * LANES]
    total = jnp.zeros((slots, LANES), jnp.float32)
    for copy, block in zip(copies, blocks):
        copy.wait()
        rows = dot(picks, rows_buffer[:, block])
        hidden[:, block] = rows.astype(jnp.bfloat16)
        scaled[:, block] = (rows * gain[:, block]).astype(jnp.bfloat16)
        for lane in range(0, COLUMNS, LANES):
            value = rows[:, lane : lane + LANES]
            total += value * value
    high = total.astype(jnp.bfloat16)
    squares[:, :LANES] = high
    squares[:, LANES:] = (total - high.astype(jnp.float32)).astype(jnp.bfloat16)


def start_pieces(pieces, buffer, copied):
    copies, first = [], 0
    for i, piece in enumerate(pieces):
        rows = pl.ds(first, piece.shape[0])
        copies.append(pltpu.make_async_copy(piece, buffer.at[rows], copied.at[i]))
        copies[-1].start()
        first += piece.shape[0]
    return copies


def forward_body(count, with_squares, scaled, *refs):
    pieces, refs = refs[:count], refs[count:]
    if with_squares:
        squares, refs = refs[0], refs[1:]
    _, out, _, rows_buffer, buffer, copied = refs
    rows = pltpu.make_async_copy(scaled, rows_buffer, copied.at[count])
    rows.start()
    copies = start_pieces(pieces, buffer, copied)
    if with_squares:
        out[:, buffer.shape[0] :] = squares[...]
    rows.wait()
    first = 0
    for piece, copy in zip(pieces, copies):
        copy.wait()
        part = slice(first, first + piece.shape[0])
        out[:, part] = contract_last(rows_buffer[...], buffer[part]).astype(out.dtype)
        first += piece.shape[0]


def scale_of(shares, width):
    total = jnp.zeros((shares[0].shape[0], LANES), jnp.float32)
    for share in shares:
        end = share.shape[1]
        for lanes in (slice(end - 2 * LANES, end - LANES), slice(end - LANES, end)):
            total += share[:, lanes].astype(jnp.float32)
    return lax.rsqrt(jnp.sum(total, axis=1, keepdims=True) / width + EPSILON)


def target_at(places, i, targets):
    distance, block = places[0, i], places[1, i]
    value = targets[0][block]
    for d in range(1, len(targets)):
        value = jnp.where(distance == d, targets[d][block], value)
    return value.astype(jnp.float32)


def residual_of(places, scale, shares, targets, inner, residual, first=0, last=None):
    last = residual.shape[1] // LANES if last is None else last
    for i in range(first, last):
        lanes = slice((i - first) * LANES, (i - first + 1) * LANES)
        value = shares[0][:, lanes].astype(jnp.float32)
        for share in shares[1:]:
            value += share[:, lanes].astype(jnp.float32)
        value *= scale
        rounded = (value - target_at(places, i, targets)).astype(jnp.bfloat16)
        residual[:, i * LANES : (i + 1) * LANES] = rounded
        inner = inner + rounded.astype(jnp.float32) * value
    return inner


def back_body(count, shared, features, narrow, width, before, places, *refs):
    pieces, refs = refs[:count], refs[count:]
    shares = []
    for size in shared:
        shares.append(refs[:size])
        refs = refs[size:]
    targets, refs = refs[:narrow], refs[narrow:]
    if before:
        back_in, inner_in, scale_in, refs = *refs[:3], refs[3:]
    _, back_out, inner_out, *scale_out, _, residual, buffer, copied = refs
    copies = start_pieces(pieces, buffer, copied)
    if before:
        scale, inner = scale_in[:, :1], inner_in[...]
    else:
        scale, inner = scale_of(shares[0], width), jnp.zeros(inner_out.shape, jnp.float32)
        scale_out[0][...] = jnp.broadcast_to(scale, scale_out[0].shape)
    first = 0
    for group, size in zip(shares, features):
        last = first + size // LANES
        inner = residual_of(places, scale, group, targets, inner, residual, first, last)
        first = last
    inner_out[...] = inner
    for copy in copies:
        copy.wait()
    for at in range(0, back_out.shape[1], COLUMNS):
        part = slice(at, at + COLUMNS)
        value = dot(residual[...], buffer[:, part])
        back_out[:, part] = value + back_in[:, part] if before else value


def tail_body(count, shared, narrow, width, places, *refs):
    pieces, refs = refs[:count], refs[count:]
    shares, refs = refs[:shared], refs[shared:]
    targets, refs = refs[:narrow], refs[narrow:]
    back_in, inner_in, scale, hidden, gain, place, table_grad, residual, factor = refs

    @pl.when(pl.program_id(0) == 0)
    def _():
        inner = residual_of(places, scale[:, :1], shares, targets, inner_in[...], residual)
        inner = jnp.sum(inner, axis=1, keepdims=True)
        factor[...] = scale[...] * scale[...] * (inner / width)

    back, first = back_in[...], 0
    for piece in pieces:
        back += dot(residual[:, first : first + piece.shape[0]], piece[...])
        first += piece.shape[0]
    row_grad = scale[:, :1] * (back * gain[...]) - hidden[...].astype(jnp.float32) * factor[:, :1]
    table_grad[...] = dot(place[...], row_grad.astype(jnp.bfloat16)).astype(jnp.bfloat16)


def whole_block(shape):
    return pl.BlockSpec(shape, lambda i, *_: (0,) * len(shape))


def column_block(rows):
    return pl.BlockSpec((rows, COLUMNS), lambda i, *_: (0, i))


def exchange_narrow(value, distance):
    narrow = lax.axis_size("narrow")
    return lax.ppermute(value, "narrow", [(i, i ^ distance) for i in range(narrow)])


def in_one_step(value):
    return [value] + [exchange_narrow(value, d) for d in range(1, lax.axis_size("narrow"))]


def in_two_steps(value):
    half = value.astype(jnp.float32) + exchange_narrow(value, 1).astype(jnp.float32)
    half = half.astype(jnp.bfloat16)
    return [half, exchange_narrow(half, 2)]


class Device:
    def __init__(self, token_shard, token_row, table, gain, kv_target):
        self.tokens = (token_shard, token_row, kv_target)
        self.table = table
        self.gain = gain.reshape(1, table.shape[1])
        self.owners = lax.axis_size(HOLDERS)
        self.slot_count = 2 * kv_target.shape[0] // self.owners
        self.slots = self.owners * self.slot_count
        self.blocks = kv_target.shape[1] // LANES
        self.width_all = table.shape[1] * lax.axis_size("narrow")
        self.before = ()

    def ask(self):
        token_shard, token_row, target = self.tokens
        tokens, width = target.shape
        sent = local_kernel(
            functools.partial(slots_body, self.slot_count),
            jax.ShapeDtypeStruct((self.slots, width + LANES), jnp.bfloat16),
        )(token_shard.reshape(1, tokens), token_row.reshape(1, tokens), target)
        self.arrived = lax.all_to_all(
            sent.reshape(self.owners, self.slot_count, width + LANES),
            HOLDERS,
            split_axis=0,
            concat_axis=0,
            tiled=True,
        ).reshape(self.slots, width + LANES)

    def pick(self, after):
        vocab_rows, width = self.table.shape
        rows = jax.ShapeDtypeStruct((self.slots, width), jnp.bfloat16)
        self.hidden, self.scaled, self.squares, target, self.place = local_kernel(
            pick_body,
            (
                rows,
                rows,
                jax.ShapeDtypeStruct((self.slots, 2 * LANES), jnp.bfloat16),
                jax.ShapeDtypeStruct((self.blocks, self.slots, LANES), jnp.bfloat16),
                jax.ShapeDtypeStruct((vocab_rows, self.slots), jnp.bfloat16),
            ),
            in_specs=in_vmem(1) + in_hbm(1) + in_vmem(1) + in_hbm(1),
            scratch_shapes=[
                pltpu.VMEM((vocab_rows, width), jnp.bfloat16),
                pltpu.SemaphoreType.DMA((width // COLUMNS,)),
            ],
        )(self.arrived, self.table, self.gain, after)
        self.target = target

    def share_targets(self):
        self.targets = in_one_step(self.target)

    def forward(self, group, after, with_squares=False):
        count = len(group)
        features = sum(piece.shape[0] for _, piece in group)
        slots, width = self.scaled.shape
        squares = [self.squares] if with_squares else []
        out_width = features + 2 * LANES * len(squares)
        return local_kernel(
            functools.partial(forward_body, count, with_squares),
            (jax.ShapeDtypeStruct((slots, out_width), jnp.bfloat16), TOKEN),
            in_specs=in_hbm(1 + count) + in_vmem(len(squares)) + in_hbm(1),
            out_specs=in_vmem(1) + in_hbm(1),
            scratch_shapes=[
                pltpu.VMEM((slots, width), jnp.bfloat16),
                pltpu.VMEM((features, width), jnp.bfloat16),
                pltpu.SemaphoreType.DMA((count + 1,)),
            ],
        )(self.scaled, *[piece for _, piece in group], *squares, after)

    def places(self, group):
        at = [which + i for which, piece in group for i in range(piece.shape[0] // LANES)]
        at = jnp.stack(at)
        distance = (at // self.blocks) ^ lax.axis_index("narrow")
        return jnp.stack([distance, at % self.blocks])

    def back(self, group, after, *shares):
        slots, width = self.scaled.shape
        count, narrow = len(group), len(self.targets)
        features = sum(piece.shape[0] for _, piece in group)
        lanes = jax.ShapeDtypeStruct((slots, LANES), jnp.float32)
        firsts = 0 if self.before else 1
        sizes = [share[0].shape[1] for share in shares]
        sizes[0] -= 2 * LANES * firsts
        back, inner, *scale, token = local_kernel(
            functools.partial(
                back_body, count, [len(share) for share in shares], sizes, narrow, self.width_all, not firsts
            ),
            [jax.ShapeDtypeStruct((slots, width), jnp.float32)] + [lanes] * (1 + firsts) + [TOKEN],
            in_specs=[pl.BlockSpec(memory_space=pltpu.SMEM)]
            + in_hbm(count)
            + in_vmem(sum(len(share) for share in shares) + narrow + len(self.before))
            + in_hbm(1),
            out_specs=in_vmem(2 + firsts) + in_hbm(1),
            scratch_shapes=[
                pltpu.VMEM((slots, features), jnp.bfloat16),
                pltpu.VMEM((features, width), jnp.bfloat16),
                pltpu.SemaphoreType.DMA((count,)),
            ],
        )(
            self.places(group),
            *[piece for _, piece in group],
            *[value for share in shares for value in share],
            *self.targets,
            *self.before,
            after,
        )
        self.before = (back, inner, *(scale or self.before[2:]))
        return token

    def tail(self, group, shares):
        slots, width = self.scaled.shape
        vocab_rows = self.place.shape[0]
        count, narrow = len(group), len(self.targets)
        features = sum(piece.shape[0] for _, piece in group)
        lanes = whole_block((slots, LANES))
        return local_kernel(
            functools.partial(tail_body, count, len(shares), narrow, self.width_all),
            jax.ShapeDtypeStruct((vocab_rows, width), jnp.bfloat16),
            grid_spec=pltpu.PrefetchScalarGridSpec(
                num_scalar_prefetch=1,
                grid=(width // COLUMNS,),
                in_specs=[column_block(piece.shape[0]) for _, piece in group]
                + [whole_block(share.shape) for share in shares]
                + [whole_block(self.target.shape)] * narrow
                + [column_block(slots), lanes, lanes, column_block(slots), column_block(1)]
                + [whole_block(self.place.shape)],
                out_specs=column_block(vocab_rows),
                scratch_shapes=[
                    pltpu.VMEM((slots, features), jnp.bfloat16),
                    pltpu.VMEM((slots, LANES), jnp.float32),
                ],
            ),
        )(
            self.places(group),
            *[piece for _, piece in group],
            *shares,
            *self.targets,
            *self.before,
            self.hidden,
            self.gain,
            self.place,
        )


def plain_order(device, weight):
    device.ask()
    device.pick(weight)
    device.share_targets()
    whole = lax.all_gather(weight, HOLDERS, axis=0, tiled=True)
    size = 4 * LANES
    groups = [
        [(jnp.int32(at // LANES), whole[at : at + size])] for at in range(0, whole.shape[0], size)
    ]
    token = weight
    for i, group in enumerate(groups[:-1]):
        projected, token = device.forward(group, token, i == 0)
        token = device.back(group, token, in_two_steps(projected))
    return device.tail(groups[-1], in_two_steps(device.forward(groups[-1], token)[0]))


def ring_order(device, weight):
    section, wide = lax.axis_index("section"), lax.axis_index("wide")
    holders = lax.axis_size(HOLDERS)
    at_ring = [i if i < holders // 2 else holders + holders // 2 - 1 - i for i in range(holders)]
    ring = jnp.where(section == 0, wide, holders - 1 - wide)

    def send(value, step):
        pairs = [(at_ring[i], at_ring[(i + step) % holders]) for i in range(holders)]
        return lax.ppermute(value, HOLDERS, pairs)

    def named(distance, piece, half=0):
        at = (ring + distance) % holders
        holder = jnp.where(at < holders // 2, at, holders + holders // 2 - 1 - at)
        return 2 * holder + half, piece

    up, down = send(weight, 1), send(weight, -1)
    device.ask()

    (up, down), token = gate([up, down], device.arrived)
    near = [named(0, weight), named(-1, up), named(1, down)]
    up, down = send(up, 1), send(down, -1)
    device.pick(token)
    sum0, done = device.forward(near, token, True)
    shares0 = in_two_steps(sum0)

    (up, down, device.target), token = gate([up, down, device.target], done)
    second = [named(-2, up), named(2, down)]
    up, down = send(up, 1), send(down, -1)
    device.share_targets()
    sum1, done = device.forward(second, token)
    shares1 = in_two_steps(sum1)

    third = [named(-3, up), named(3, down)]
    up, down, token = gate_halves(up, down, done, *device.targets)
    up, down = send(up, 1), send(down, -1)
    sum2, done = device.forward(third, token)
    shares2 = in_one_step(sum2)
    done = device.back(near + second, done, shares0, shares1)

    (up, down), token = gate([up, down], done)
    last = [named(4, up), named(4, down, 1)]
    sum3, done = device.forward(last, token)
    shares3 = in_one_step(sum3)
    device.back(third, done, shares2)
    return device.tail(last, shares3)


def on_device(token_shard, token_row, table, gain, key_value_weight, kv_target):
    device = Device(token_shard, token_row, table, gain, kv_target)
    holders = (lax.axis_size("section"), lax.axis_size("wide"))
    if holders == (2, 4) and key_value_weight.shape[0] == 2 * LANES:
        return ring_order(device, key_value_weight)
    return plain_order(device, key_value_weight)


def solution(mesh):
    return jax.shard_map(
        on_device,
        mesh=mesh,
        in_specs=(
            P(("section", "wide"), None),
            P(("section", "wide")),
            P(("section", "wide"), "narrow"),
            P("narrow"),
            P(("section", "wide"), "narrow"),
            P(("section", "wide"), "narrow"),
        ),
        out_specs=P(("section", "wide"), "narrow"),
        check_vma=False,
    )
```

```python
import functools

import jax
import jax.numpy as jnp
from jax import lax
from jax.experimental import pallas as pl
from jax.experimental.pallas import tpu as pltpu
from jax.sharding import PartitionSpec as P

EPSILON = 1e-05

HOLDERS = ("section", "wide")
LANES = 128
COLUMNS = 512
SMALL_COST = pl.CostEstimate(flops=1000, bytes_accessed=1000, transcendentals=0)


def contract_last(left, right):
    return lax.dot_general(
        left, right, (((1,), (1,)), ((), ())), preferred_element_type=jnp.float32
    )


def dot(left, right):
    return jnp.dot(left, right, preferred_element_type=jnp.float32)


VMEM_BYTES = 63 * 1024 * 1024
END_VMEM_BYTES = 24 * 1024 * 1024


def local_kernel(body, out_shape, vmem_bytes=VMEM_BYTES, **kwargs):
    return pl.pallas_call(
        body,
        out_shape=out_shape,
        compiler_params=pltpu.CompilerParams(vmem_limit_bytes=vmem_bytes),
        cost_estimate=SMALL_COST,
        **kwargs,
    )


def in_hbm(count):
    return [pl.BlockSpec(memory_space=pltpu.HBM)] * count


TOKEN = jax.ShapeDtypeStruct((8, LANES), jnp.float32)


def gate(values, *after):
    count = len(values)
    *values, token = local_kernel(
        lambda *refs: None,
        [jax.ShapeDtypeStruct(v.shape, v.dtype) for v in values] + [TOKEN],
        in_specs=in_hbm(count + len(after)),
        out_specs=in_hbm(count + 1),
        input_output_aliases={i: i for i in range(count)},
    )(*values, *after)
    return values, token


def halves_body(up, down, *refs):
    up_half, down_half, _, buffer, copied = refs[-5:]
    rows = up_half.shape[0]
    ends = [(up.at[pl.ds(0, rows)], up_half), (down.at[pl.ds(rows, rows)], down_half)]
    copies = [
        [
            pltpu.make_async_copy(source, buffer.at[i], copied.at[2 * i]),
            pltpu.make_async_copy(buffer.at[i], result, copied.at[2 * i + 1]),
        ]
        for i, (source, result) in enumerate(ends)
    ]
    for first, _ in copies:
        first.start()
    for first, second in copies:
        first.wait()
        second.start()
    for _, second in copies:
        second.wait()


def gate_halves(up, down, *after):
    half = jax.ShapeDtypeStruct((up.shape[0] // 2, up.shape[1]), up.dtype)
    return local_kernel(
        halves_body,
        [half, half, TOKEN],
        in_specs=in_hbm(2 + len(after)),
        out_specs=in_hbm(3),
        scratch_shapes=[
            pltpu.VMEM((2, *half.shape), half.dtype),
            pltpu.SemaphoreType.DMA((4,)),
        ],
    )(up, down, *after)


def in_vmem(count):
    return [pl.BlockSpec(memory_space=pltpu.VMEM)] * count


def slots_body(slot_count, shard_row, token_row, target, sent):
    tokens, width = target.shape
    slots = sent.shape[0]
    shard_here = shard_row[...]
    earlier = lax.broadcasted_iota(jnp.int32, (tokens, tokens), 0) < lax.broadcasted_iota(
        jnp.int32, (tokens, tokens), 1
    )
    shard_column = jnp.broadcast_to(shard_here.astype(jnp.float32), (tokens, tokens)).T
    same = (shard_column.astype(jnp.int32) == shard_here) & earlier
    rank = jnp.sum(jnp.where(same, 1.0, 0.0), axis=0, keepdims=True).astype(jnp.int32)
    position = shard_here * slot_count + rank
    here = lax.broadcasted_iota(jnp.int32, (slots, tokens), 0) == position
    to_slot = jnp.where(here, 1.0, 0.0)
    sent[:, :width] = dot(to_slot.astype(jnp.bfloat16), target[...]).astype(jnp.bfloat16)
    row = token_row[...]
    high = jnp.sum(to_slot * (row >> 8).astype(jnp.float32), axis=1, keepdims=True)
    low = jnp.sum(to_slot * (row & 255).astype(jnp.float32), axis=1, keepdims=True)
    taken = jnp.sum(to_slot, axis=1, keepdims=True)
    lane = lax.broadcasted_iota(jnp.int32, (slots, LANES), 1)
    numbers = jnp.where(
        lane == 0, high, jnp.where(lane == 1, low, jnp.where(lane == 2, taken, 0.0))
    )
    sent[:, width:] = numbers.astype(jnp.bfloat16)


def squares_body(table, _, squares, rows_buffer, copied):
    vocab_rows, width = table.shape
    count = copied.shape[0]
    per_copy = vocab_rows // count
    copies = []
    for i in range(count):
        rows = pl.ds(i * per_copy, per_copy)
        copies.append(pltpu.make_async_copy(table.at[rows], rows_buffer.at[rows], copied.at[i]))
        copies[-1].start()
    for i, copy in enumerate(copies):
        copy.wait()
        rows = slice(i * per_copy, (i + 1) * per_copy)
        total = jnp.zeros((per_copy, LANES), jnp.float32)
        for at in range(0, width, LANES):
            value = rows_buffer[rows, at : at + LANES].astype(jnp.float32)
            total += value * value
        total = jnp.broadcast_to(jnp.sum(total, axis=1, keepdims=True), total.shape)
        squares[:, rows] = total.T[: squares.shape[0]]


def pick_body(width_all, arrived, table, gain, *refs):
    shares, refs = refs[:-8], refs[-8:]
    _, hidden, normed, scale, target, place, rows_buffer, copied = refs
    vocab_rows, width = table.shape
    target_width = target.shape[0] * LANES
    blocks = [slice(at, at + COLUMNS) for at in range(0, width, COLUMNS)]
    copies = [
        pltpu.make_async_copy(table.at[:, block], rows_buffer.at[:, block], copied.at[i])
        for i, block in enumerate(blocks)
    ]
    for copy in copies:
        copy.start()
    here = arrived[...]
    slots = here.shape[0]
    numbers = here[:, target_width:].astype(jnp.float32)
    row = jnp.where(numbers[:, 2:3] > 0.5, numbers[:, 0:1] * 256.0 + numbers[:, 1:2], -1.0)
    picks = jnp.where(
        row.astype(jnp.int32) == lax.broadcasted_iota(jnp.int32, (slots, vocab_rows), 1), 1.0, 0.0
    )
    total = shares[0][:1]
    for share in shares[1:]:
        total += share[:1]
    row_scale = jnp.sum(picks * lax.rsqrt(total / width_all + EPSILON), axis=1, keepdims=True)
    scale[...] = jnp.broadcast_to(row_scale, scale.shape)
    place[...] = picks.T.astype(jnp.bfloat16)
    picks = picks.astype(jnp.bfloat16)
    for i in range(target.shape[0]):
        target[i] = here[:, i * LANES : (i + 1) * LANES]
    for copy, block in zip(copies, blocks):
        copy.wait()
        rows = dot(picks, rows_buffer[:, block])
        hidden[:, block] = rows.astype(jnp.bfloat16)
        normed[:, block] = (rows * row_scale * gain[:, block]).astype(jnp.bfloat16)


def start_pieces(pieces, buffer, copied):
    copies, first = [], 0
    for i, piece in enumerate(pieces):
        rows = pl.ds(first, piece.shape[0])
        copies.append(pltpu.make_async_copy(piece, buffer.at[rows], copied.at[i]))
        copies[-1].start()
        first += piece.shape[0]
    return copies


def forward_body(count, normed, *refs):
    pieces, refs = refs[:count], refs[count:]
    _, out, _, rows_buffer, buffer, copied = refs
    rows = pltpu.make_async_copy(normed, rows_buffer, copied.at[count])
    rows.start()
    copies = start_pieces(pieces, buffer, copied)
    rows.wait()
    first = last = 0
    for piece, copy in zip(pieces, copies):
        copy.wait()
        last += piece.shape[0]
        if last - first >= 2 * LANES or last == buffer.shape[0]:
            part = slice(first, last)
            out[:, part] = contract_last(rows_buffer[...], buffer[part]).astype(out.dtype)
            first = last


def target_at(places, i, targets):
    distance, block = places[0, i], places[1, i]
    value = targets[0][block]
    for d in range(1, len(targets)):
        value = jnp.where(distance == d, targets[d][block], value)
    return value.astype(jnp.float32)


def residual_of(places, shares, targets, inner, residual, first=0, last=None):
    last = residual.shape[1] // LANES if last is None else last
    for i in range(first, last):
        lanes = slice((i - first) * LANES, (i - first + 1) * LANES)
        value = shares[0][:, lanes].astype(jnp.float32)
        for share in shares[1:]:
            value += share[:, lanes].astype(jnp.float32)
        rounded = (value - target_at(places, i, targets)).astype(jnp.bfloat16)
        residual[:, i * LANES : (i + 1) * LANES] = rounded
        inner = inner + rounded.astype(jnp.float32) * value
    return inner


def back_body(count, shared, features, narrow, before, ahead, places, *refs):
    pieces, refs = refs[:count], refs[count:]
    shares = []
    for size in shared:
        shares.append(refs[:size])
        refs = refs[size:]
    targets, refs = refs[:narrow], refs[narrow:]
    if before:
        back_in, inner_in, refs = refs[0], refs[1], refs[2:]
    _, back_out, inner_out, *target_out, _, residual, buffer, copied = refs
    copies = start_pieces(pieces, buffer, copied)
    inner = inner_in[...] if before else jnp.zeros(inner_out.shape, jnp.float32)
    first = 0
    for group, size in zip(shares, features):
        last = first + size // LANES
        inner = residual_of(places, group, targets, inner, residual, first, last)
        first = last
    inner_out[...] = inner
    for i in range(ahead):
        lanes = slice(i * LANES, (i + 1) * LANES)
        target_out[0][:, lanes] = target_at(places, first + i, targets).astype(jnp.bfloat16)
    for copy in copies:
        copy.wait()
    for at in range(0, back_out.shape[1], COLUMNS):
        part = slice(at, at + COLUMNS)
        value = dot(residual[...], buffer[:, part])
        back_out[:, part] = value + back_in[:, part] if before else value


def tail_body(count, width, *refs):
    pieces, refs = refs[:count], refs[count:]
    shares, refs = refs[:-12], refs[-12:]
    target, back_in, inner_in, hidden, gain, scale, place, table_grad, *refs = refs
    residual, buffer, row_grad, copied = refs
    inner = inner_in[...]
    for at in range(0, residual.shape[1], LANES):
        lanes = slice(at, at + LANES)
        value = shares[0][:, lanes].astype(jnp.float32)
        for share in shares[1:]:
            value += share[:, lanes].astype(jnp.float32)
        rounded = (value - target[:, lanes].astype(jnp.float32)).astype(jnp.bfloat16)
        residual[:, lanes] = rounded
        inner += rounded.astype(jnp.float32) * value
    row_scale = scale[:, :1]
    factor = row_scale * row_scale * (jnp.sum(inner, axis=1, keepdims=True) / width)
    copies = []
    for i in range(copied.shape[0]):
        block = slice(i * COLUMNS, (i + 1) * COLUMNS)
        back, first = back_in[:, block], 0
        weights = jnp.concatenate([piece[:, block] for piece in pieces], axis=0)
        back += dot(residual[...], weights)
        row_grad[...] = (
            row_scale * (back * gain[:, block]) - hidden[:, block].astype(jnp.float32) * factor
        ).astype(jnp.bfloat16)
        buffer[i] = dot(place[...], row_grad[...]).astype(jnp.bfloat16)
        copies.append(pltpu.make_async_copy(buffer.at[i], table_grad.at[:, block], copied.at[i]))
        copies[-1].start()
    for copy in copies:
        copy.wait()


def exchange_narrow(value, distance):
    narrow = lax.axis_size("narrow")
    return lax.ppermute(value, "narrow", [(i, i ^ distance) for i in range(narrow)])


def in_one_step(value):
    return [value] + [exchange_narrow(value, d) for d in range(1, lax.axis_size("narrow"))]


def in_two_steps(value):
    half = value.astype(jnp.float32) + exchange_narrow(value, 1).astype(jnp.float32)
    half = half.astype(jnp.bfloat16)
    return [half, exchange_narrow(half, 2)]


class Device:
    def __init__(self, token_shard, token_row, table, gain, kv_target):
        self.tokens = (token_shard, token_row, kv_target)
        self.table = table
        self.gain = gain.reshape(1, table.shape[1])
        self.owners = lax.axis_size(HOLDERS)
        self.slot_count = 2 * kv_target.shape[0] // self.owners
        self.slots = self.owners * self.slot_count
        self.blocks = kv_target.shape[1] // LANES
        self.width_all = table.shape[1] * lax.axis_size("narrow")
        self.before = ()

    def ask(self):
        token_shard, token_row, target = self.tokens
        tokens, width = target.shape
        self.sent = local_kernel(
            functools.partial(slots_body, self.slot_count),
            jax.ShapeDtypeStruct((self.slots, width + LANES), jnp.bfloat16),
        )(token_shard.reshape(1, tokens), token_row.reshape(1, tokens), target)
        self.arrived = lax.all_to_all(
            self.sent.reshape(self.owners, self.slot_count, width + LANES),
            HOLDERS,
            split_axis=0,
            concat_axis=0,
            tiled=True,
        ).reshape(self.slots, width + LANES)

    def square(self, after):
        vocab_rows, width = self.table.shape
        squares = local_kernel(
            squares_body,
            jax.ShapeDtypeStruct((8, vocab_rows), jnp.float32),
            in_specs=in_hbm(2),
            scratch_shapes=[
                pltpu.VMEM((vocab_rows, width), jnp.bfloat16),
                pltpu.SemaphoreType.DMA((vocab_rows // LANES,)),
            ],
        )(self.table, after)
        self.squares = in_one_step(squares)

    def pick(self, after):
        vocab_rows, width = self.table.shape
        rows = jax.ShapeDtypeStruct((self.slots, width), jnp.bfloat16)
        self.hidden, self.normed, self.scale, self.target, self.place = local_kernel(
            functools.partial(pick_body, self.width_all),
            (
                rows,
                rows,
                jax.ShapeDtypeStruct((self.slots, LANES), jnp.float32),
                jax.ShapeDtypeStruct((self.blocks, self.slots, LANES), jnp.bfloat16),
                jax.ShapeDtypeStruct((vocab_rows, self.slots), jnp.bfloat16),
            ),
            in_specs=in_vmem(1) + in_hbm(1) + in_vmem(1 + len(self.squares)) + in_hbm(1),
            scratch_shapes=[
                pltpu.VMEM((vocab_rows, width), jnp.bfloat16),
                pltpu.SemaphoreType.DMA((width // COLUMNS,)),
            ],
        )(self.arrived, self.table, self.gain, *self.squares, after)

    def share_targets(self):
        self.targets = in_one_step(self.target)

    def forward(self, group, after, vmem_bytes=VMEM_BYTES):
        count = len(group)
        features = sum(piece.shape[0] for _, piece in group)
        slots, width = self.normed.shape
        return local_kernel(
            functools.partial(forward_body, count),
            (jax.ShapeDtypeStruct((slots, features), jnp.bfloat16), TOKEN),
            vmem_bytes=vmem_bytes,
            in_specs=in_hbm(2 + count),
            out_specs=in_vmem(1) + in_hbm(1),
            scratch_shapes=[
                pltpu.VMEM((slots, width), jnp.bfloat16),
                pltpu.VMEM((features, width), jnp.bfloat16),
                pltpu.SemaphoreType.DMA((count + 1,)),
            ],
        )(self.normed, *[piece for _, piece in group], after)

    def places(self, group):
        at = [which + i for which, piece in group for i in range(piece.shape[0] // LANES)]
        at = jnp.stack(at)
        distance = (at // self.blocks) ^ lax.axis_index("narrow")
        return jnp.stack([distance, at % self.blocks])

    def back(self, group, after, *shares, ahead=(), vmem_bytes=VMEM_BYTES):
        slots, width = self.normed.shape
        count, narrow = len(group), len(self.targets)
        features = sum(piece.shape[0] for _, piece in group)
        lanes = jax.ShapeDtypeStruct((slots, LANES), jnp.float32)
        blocks_ahead = sum(piece.shape[0] for _, piece in ahead) // LANES
        targets = [jax.ShapeDtypeStruct((slots, blocks_ahead * LANES), jnp.bfloat16)]
        targets = targets if ahead else []
        sizes = [share[0].shape[1] for share in shares]
        shared = [len(share) for share in shares]
        back, inner, *targets, token = local_kernel(
            functools.partial(
                back_body, count, shared, sizes, narrow, len(self.before) > 0, blocks_ahead
            ),
            [jax.ShapeDtypeStruct((slots, width), jnp.float32), lanes] + targets + [TOKEN],
            vmem_bytes=vmem_bytes,
            in_specs=[pl.BlockSpec(memory_space=pltpu.SMEM)]
            + in_hbm(count)
            + in_vmem(sum(shared) + narrow + len(self.before))
            + in_hbm(1),
            out_specs=in_vmem(2 + len(targets)) + in_hbm(1),
            scratch_shapes=[
                pltpu.VMEM((slots, features), jnp.bfloat16),
                pltpu.VMEM((features, width), jnp.bfloat16),
                pltpu.SemaphoreType.DMA((count,)),
            ],
        )(
            self.places(group + list(ahead)),
            *[piece for _, piece in group],
            *[value for share in shares for value in share],
            *self.targets,
            *self.before,
            after,
        )
        self.before = (back, inner)
        self.last_target = targets
        return token

    def tail(self, group, shares):
        slots, width = self.normed.shape
        vocab_rows = self.place.shape[0]
        count = len(group)
        features = sum(piece.shape[0] for _, piece in group)
        return local_kernel(
            functools.partial(tail_body, count, self.width_all),
            jax.ShapeDtypeStruct((vocab_rows, width), jnp.bfloat16),
            vmem_bytes=END_VMEM_BYTES,
            in_specs=in_vmem(count + len(shares) + 7),
            out_specs=in_hbm(1)[0],
            scratch_shapes=[
                pltpu.VMEM((slots, features), jnp.bfloat16),
                pltpu.VMEM((width // COLUMNS, vocab_rows, COLUMNS), jnp.bfloat16),
                pltpu.VMEM((slots, COLUMNS), jnp.bfloat16),
                pltpu.SemaphoreType.DMA((width // COLUMNS,)),
            ],
        )(
            *[piece for _, piece in group],
            *shares,
            *self.last_target,
            *self.before,
            self.hidden,
            self.gain,
            self.scale,
            self.place,
        )


def plain_order(device, weight):
    device.ask()
    device.square(device.sent)
    device.pick(weight)
    device.share_targets()
    whole = lax.all_gather(weight, HOLDERS, axis=0, tiled=True)
    size = 4 * LANES
    groups = [
        [(jnp.int32(at // LANES), whole[at : at + size])] for at in range(0, whole.shape[0], size)
    ]
    token = weight
    for i, group in enumerate(groups[:-1]):
        projected, token = device.forward(group, token)
        ahead = groups[-1] if i == len(groups) - 2 else ()
        token = device.back(group, token, in_two_steps(projected), ahead=ahead)
    return device.tail(groups[-1], in_two_steps(device.forward(groups[-1], token)[0]))


def ring_order(device, weight):
    section, wide = lax.axis_index("section"), lax.axis_index("wide")
    holders = lax.axis_size(HOLDERS)
    at_ring = [i if i < holders // 2 else holders + holders // 2 - 1 - i for i in range(holders)]
    ring = jnp.where(section == 0, wide, holders - 1 - wide)

    def send(value, step):
        pairs = [(at_ring[i], at_ring[(i + step) % holders]) for i in range(holders)]
        return lax.ppermute(value, HOLDERS, pairs)

    def named(distance, piece, half=0):
        at = (ring + distance) % holders
        holder = jnp.where(at < holders // 2, at, holders + holders // 2 - 1 - at)
        return 2 * holder + half, piece

    up, down = send(weight, 1), send(weight, -1)
    device.ask()
    device.square(device.sent)

    (up, down), token = gate([up, down], device.arrived)
    near = [named(0, weight), named(-1, up), named(1, down)]
    up, down = send(up, 1), send(down, -1)
    device.pick(token)
    sum0, done = device.forward(near, token)
    shares0 = in_two_steps(sum0)

    (up, down, device.target), token = gate([up, down, device.target], done)
    second = [named(-2, up), named(2, down)]
    up, down = send(up, 1), send(down, -1)
    device.share_targets()
    sum1, done = device.forward(second, token)
    shares1 = in_two_steps(sum1)

    third = [named(-3, up), named(3, down)]
    up, down, token = gate_halves(up, down, done, *device.targets)
    up, down = send(up, 1), send(down, -1)
    sum2, done = device.forward(third, token, END_VMEM_BYTES)
    shares2 = in_one_step(sum2)
    done = device.back(near + second, done, shares0, shares1, vmem_bytes=END_VMEM_BYTES)

    last = [named(4, up), named(4, down, 1)]
    sum3, done = device.forward(last, done, END_VMEM_BYTES)
    shares3 = in_one_step(sum3)
    device.back(third, done, shares2, ahead=last, vmem_bytes=END_VMEM_BYTES)
    return device.tail(last, shares3)


def on_device(token_shard, token_row, table, gain, key_value_weight, kv_target):
    device = Device(token_shard, token_row, table, gain, kv_target)
    holders = (lax.axis_size("section"), lax.axis_size("wide"))
    if holders == (2, 4) and key_value_weight.shape[0] == 2 * LANES:
        return ring_order(device, key_value_weight)
    return plain_order(device, key_value_weight)


def solution(mesh):
    return jax.shard_map(
        on_device,
        mesh=mesh,
        in_specs=(
            P(("section", "wide"), None),
            P(("section", "wide")),
            P(("section", "wide"), "narrow"),
            P("narrow"),
            P(("section", "wide"), "narrow"),
            P(("section", "wide"), "narrow"),
        ),
        out_specs=P(("section", "wide"), "narrow"),
        check_vma=False,
    )
```

```python
import functools

import jax
import jax.numpy as jnp
from jax import lax
from jax.experimental import pallas as pl
from jax.experimental.pallas import tpu as pltpu
from jax.sharding import PartitionSpec as P

EPSILON = 1e-05

HOLDERS = ("section", "wide")
LANES = 128
COLUMNS = 512
SMALL_COST = pl.CostEstimate(flops=1000, bytes_accessed=1000, transcendentals=0)


def contract_last(left, right):
    return lax.dot_general(
        left, right, (((1,), (1,)), ((), ())), preferred_element_type=jnp.float32
    )


def dot(left, right):
    return jnp.dot(left, right, preferred_element_type=jnp.float32)


VMEM_BYTES = 63 * 1024 * 1024
END_VMEM_BYTES = 24 * 1024 * 1024


def local_kernel(body, out_shape, vmem_bytes=VMEM_BYTES, **kwargs):
    return pl.pallas_call(
        body,
        out_shape=out_shape,
        compiler_params=pltpu.CompilerParams(vmem_limit_bytes=vmem_bytes),
        cost_estimate=SMALL_COST,
        **kwargs,
    )


def in_hbm(count):
    return [pl.BlockSpec(memory_space=pltpu.HBM)] * count


def anywhere(count):
    return [pl.BlockSpec(memory_space=pl.ANY)] * count


TOKEN = jax.ShapeDtypeStruct((8, LANES), jnp.float32)


def gate(values, *after):
    count = len(values)
    *values, token = local_kernel(
        lambda *refs: None,
        [jax.ShapeDtypeStruct(v.shape, v.dtype) for v in values] + [TOKEN],
        in_specs=in_hbm(count + len(after)),
        out_specs=in_hbm(count + 1),
        input_output_aliases={i: i for i in range(count)},
    )(*values, *after)
    return values, token


def in_vmem(count):
    return [pl.BlockSpec(memory_space=pltpu.VMEM)] * count


def slots_body(slot_count, shard_row, token_row, target, sent):
    tokens, width = target.shape
    slots = sent.shape[0]
    shard_here = shard_row[...]
    earlier = lax.broadcasted_iota(jnp.int32, (tokens, tokens), 0) < lax.broadcasted_iota(
        jnp.int32, (tokens, tokens), 1
    )
    shard_column = jnp.broadcast_to(shard_here.astype(jnp.float32), (tokens, tokens)).T
    same = (shard_column.astype(jnp.int32) == shard_here) & earlier
    rank = jnp.sum(jnp.where(same, 1.0, 0.0), axis=0, keepdims=True).astype(jnp.int32)
    position = shard_here * slot_count + rank
    here = lax.broadcasted_iota(jnp.int32, (slots, tokens), 0) == position
    to_slot = jnp.where(here, 1.0, 0.0)
    sent[:, :width] = dot(to_slot.astype(jnp.bfloat16), target[...]).astype(jnp.bfloat16)
    row = token_row[...]
    high = jnp.sum(to_slot * (row >> 8).astype(jnp.float32), axis=1, keepdims=True)
    low = jnp.sum(to_slot * (row & 255).astype(jnp.float32), axis=1, keepdims=True)
    taken = jnp.sum(to_slot, axis=1, keepdims=True)
    lane = lax.broadcasted_iota(jnp.int32, (slots, LANES), 1)
    numbers = jnp.where(
        lane == 0, high, jnp.where(lane == 1, low, jnp.where(lane == 2, taken, 0.0))
    )
    sent[:, width:] = numbers.astype(jnp.bfloat16)


def squares_body(table, _, squares, rows_buffer, copied):
    vocab_rows, width = table.shape
    count = copied.shape[0]
    per_copy = vocab_rows // count
    copies = []
    for i in range(count):
        rows = pl.ds(i * per_copy, per_copy)
        copies.append(pltpu.make_async_copy(table.at[rows], rows_buffer.at[rows], copied.at[i]))
        copies[-1].start()
    for i, copy in enumerate(copies):
        copy.wait()
        rows = slice(i * per_copy, (i + 1) * per_copy)
        total = jnp.zeros((per_copy, LANES), jnp.float32)
        for at in range(0, width, LANES):
            value = rows_buffer[rows, at : at + LANES].astype(jnp.float32)
            total += value * value
        total = jnp.broadcast_to(jnp.sum(total, axis=1, keepdims=True), total.shape)
        squares[:, rows] = total.T[: squares.shape[0]]


def pick_body(width_all, arrived, table, gain, *refs):
    shares, refs = refs[:-8], refs[-8:]
    _, hidden, normed, scale, target, place, rows_buffer, copied = refs
    vocab_rows, width = table.shape
    target_width = target.shape[0] * LANES
    blocks = [slice(at, at + COLUMNS) for at in range(0, width, COLUMNS)]
    copies = [
        pltpu.make_async_copy(table.at[:, block], rows_buffer.at[:, block], copied.at[i])
        for i, block in enumerate(blocks)
    ]
    for copy in copies:
        copy.start()
    here = arrived[...]
    slots = here.shape[0]
    numbers = here[:, target_width:].astype(jnp.float32)
    row = jnp.where(numbers[:, 2:3] > 0.5, numbers[:, 0:1] * 256.0 + numbers[:, 1:2], -1.0)
    picks = jnp.where(
        row.astype(jnp.int32) == lax.broadcasted_iota(jnp.int32, (slots, vocab_rows), 1), 1.0, 0.0
    )
    total = shares[0][:1]
    for share in shares[1:]:
        total += share[:1]
    row_scale = jnp.sum(picks * lax.rsqrt(total / width_all + EPSILON), axis=1, keepdims=True)
    scale[...] = jnp.broadcast_to(row_scale, scale.shape)
    place[...] = picks.T.astype(jnp.bfloat16)
    picks = picks.astype(jnp.bfloat16)
    for i in range(target.shape[0]):
        target[i] = here[:, i * LANES : (i + 1) * LANES]
    for copy, block in zip(copies, blocks):
        copy.wait()
        rows = dot(picks, rows_buffer[:, block])
        hidden[:, block] = rows.astype(jnp.bfloat16)
        normed[:, block] = (rows * row_scale * gain[:, block]).astype(jnp.bfloat16)


def start_pieces(pieces, buffer, copied):
    copies, first = [], 0
    for i, piece in enumerate(pieces):
        rows = pl.ds(first, piece.shape[0])
        copies.append(pltpu.make_async_copy(piece, buffer.at[rows], copied.at[i]))
        copies[-1].start()
        first += piece.shape[0]
    return copies


def forward_body(count, normed, *refs):
    pieces, refs = refs[:count], refs[count:]
    _, out, _, rows_buffer, buffer, copied = refs
    rows = pltpu.make_async_copy(normed, rows_buffer, copied.at[count])
    rows.start()
    copies = start_pieces(pieces, buffer, copied)
    rows.wait()
    first = last = 0
    for piece, copy in zip(pieces, copies):
        copy.wait()
        last += piece.shape[0]
        if last - first >= 2 * LANES or last == buffer.shape[0]:
            part = slice(first, last)
            out[:, part] = contract_last(rows_buffer[...], buffer[part]).astype(out.dtype)
            first = last


def target_at(places, i, targets):
    distance, block = places[0, i], places[1, i]
    value = targets[0][block]
    for d in range(1, len(targets)):
        value = jnp.where(distance == d, targets[d][block], value)
    return value.astype(jnp.float32)


def residual_of(places, shares, targets, inner, residual, first=0, last=None):
    last = residual.shape[1] // LANES if last is None else last
    for i in range(first, last):
        lanes = slice((i - first) * LANES, (i - first + 1) * LANES)
        value = shares[0][:, lanes].astype(jnp.float32)
        for share in shares[1:]:
            value += share[:, lanes].astype(jnp.float32)
        rounded = (value - target_at(places, i, targets)).astype(jnp.bfloat16)
        residual[:, i * LANES : (i + 1) * LANES] = rounded
        inner = inner + rounded.astype(jnp.float32) * value
    return inner


def back_body(count, shared, features, narrow, before, ahead, places, *refs):
    pieces, refs = refs[:count], refs[count:]
    shares = []
    for size in shared:
        shares.append(refs[:size])
        refs = refs[size:]
    targets, refs = refs[:narrow], refs[narrow:]
    if before:
        back_in, inner_in, refs = refs[0], refs[1], refs[2:]
    _, back_out, inner_out, *target_out, _, residual, buffer, copied = refs
    copies = start_pieces(pieces, buffer, copied)
    inner = inner_in[...] if before else jnp.zeros(inner_out.shape, jnp.float32)
    first = 0
    for group, size in zip(shares, features):
        last = first + size // LANES
        inner = residual_of(places, group, targets, inner, residual, first, last)
        first = last
    inner_out[...] = inner
    for i in range(ahead):
        lanes = slice(i * LANES, (i + 1) * LANES)
        target_out[0][:, lanes] = target_at(places, first + i, targets).astype(jnp.bfloat16)
    for copy in copies:
        copy.wait()
    for at in range(0, back_out.shape[1], COLUMNS):
        part = slice(at, at + COLUMNS)
        value = dot(residual[...], buffer[:, part])
        back_out[:, part] = value + back_in[:, part] if before else value


def tail_body(count, width, *refs):
    pieces, refs = refs[:count], refs[count:]
    shares, refs = refs[:-12], refs[-12:]
    target, back_in, inner_in, hidden, gain, scale, place, table_grad, *refs = refs
    residual, buffer, row_grad, copied = refs
    inner = inner_in[...]
    for at in range(0, residual.shape[1], LANES):
        lanes = slice(at, at + LANES)
        value = shares[0][:, lanes].astype(jnp.float32)
        for share in shares[1:]:
            value += share[:, lanes].astype(jnp.float32)
        rounded = (value - target[:, lanes].astype(jnp.float32)).astype(jnp.bfloat16)
        residual[:, lanes] = rounded
        inner += rounded.astype(jnp.float32) * value
    row_scale = scale[:, :1]
    factor = row_scale * row_scale * (jnp.sum(inner, axis=1, keepdims=True) / width)
    copies = []
    for i in range(copied.shape[0]):
        block = slice(i * COLUMNS, (i + 1) * COLUMNS)
        back, first = back_in[:, block], 0
        weights = jnp.concatenate([piece[:, block] for piece in pieces], axis=0)
        back += dot(residual[...], weights)
        row_grad[...] = (
            row_scale * (back * gain[:, block]) - hidden[:, block].astype(jnp.float32) * factor
        ).astype(jnp.bfloat16)
        buffer[i] = dot(place[...], row_grad[...]).astype(jnp.bfloat16)
        copies.append(pltpu.make_async_copy(buffer.at[i], table_grad.at[:, block], copied.at[i]))
        copies[-1].start()
    for copy in copies:
        copy.wait()


def exchange_narrow(value, distance):
    narrow = lax.axis_size("narrow")
    return lax.ppermute(value, "narrow", [(i, i ^ distance) for i in range(narrow)])


def in_one_step(value):
    return [value] + [exchange_narrow(value, d) for d in range(1, lax.axis_size("narrow"))]


def in_two_steps(value, first=1):
    half = value.astype(jnp.float32) + exchange_narrow(value, first).astype(jnp.float32)
    half = half.astype(jnp.bfloat16)
    return [half, exchange_narrow(half, 3 - first)]


class Device:
    def __init__(self, token_shard, token_row, table, gain, kv_target):
        self.tokens = (token_shard, token_row, kv_target)
        self.table = table
        self.gain = gain.reshape(1, table.shape[1])
        self.owners = lax.axis_size(HOLDERS)
        self.slot_count = 2 * kv_target.shape[0] // self.owners
        self.slots = self.owners * self.slot_count
        self.blocks = kv_target.shape[1] // LANES
        self.width_all = table.shape[1] * lax.axis_size("narrow")
        self.before = ()

    def ask(self):
        token_shard, token_row, target = self.tokens
        tokens, width = target.shape
        self.sent = local_kernel(
            functools.partial(slots_body, self.slot_count),
            jax.ShapeDtypeStruct((self.slots, width + LANES), jnp.bfloat16),
        )(token_shard.reshape(1, tokens), token_row.reshape(1, tokens), target)
        self.arrived = lax.all_to_all(
            self.sent.reshape(self.owners, self.slot_count, width + LANES),
            HOLDERS,
            split_axis=0,
            concat_axis=0,
            tiled=True,
        ).reshape(self.slots, width + LANES)

    def square(self, after):
        vocab_rows, width = self.table.shape
        squares = local_kernel(
            squares_body,
            jax.ShapeDtypeStruct((8, vocab_rows), jnp.float32),
            in_specs=in_hbm(2),
            scratch_shapes=[
                pltpu.VMEM((vocab_rows, width), jnp.bfloat16),
                pltpu.SemaphoreType.DMA((vocab_rows // LANES,)),
            ],
        )(self.table, after)
        self.squares = in_one_step(squares)

    def pick(self, after):
        vocab_rows, width = self.table.shape
        rows = jax.ShapeDtypeStruct((self.slots, width), jnp.bfloat16)
        self.hidden, self.normed, self.scale, self.target, self.place = local_kernel(
            functools.partial(pick_body, self.width_all),
            (
                rows,
                rows,
                jax.ShapeDtypeStruct((self.slots, LANES), jnp.float32),
                jax.ShapeDtypeStruct((self.blocks, self.slots, LANES), jnp.bfloat16),
                jax.ShapeDtypeStruct((vocab_rows, self.slots), jnp.bfloat16),
            ),
            in_specs=in_vmem(1) + in_hbm(1) + in_vmem(1 + len(self.squares)) + in_hbm(1),
            scratch_shapes=[
                pltpu.VMEM((vocab_rows, width), jnp.bfloat16),
                pltpu.SemaphoreType.DMA((width // COLUMNS,)),
            ],
        )(self.arrived, self.table, self.gain, *self.squares, after)

    def share_targets(self):
        along = exchange_narrow(self.target, 2)
        across = exchange_narrow(self.target, 1)
        self.targets = [self.target, across, along, exchange_narrow(along, 1)]

    def forward(self, group, after, vmem_bytes=VMEM_BYTES):
        count = len(group)
        features = sum(piece.shape[0] for _, piece in group)
        slots, width = self.normed.shape
        return local_kernel(
            functools.partial(forward_body, count),
            (jax.ShapeDtypeStruct((slots, features), jnp.bfloat16), TOKEN),
            vmem_bytes=vmem_bytes,
            in_specs=in_hbm(1) + anywhere(count) + in_hbm(1),
            out_specs=in_vmem(1) + in_hbm(1),
            scratch_shapes=[
                pltpu.VMEM((slots, width), jnp.bfloat16),
                pltpu.VMEM((features, width), jnp.bfloat16),
                pltpu.SemaphoreType.DMA((count + 1,)),
            ],
        )(self.normed, *[piece for _, piece in group], after)

    def places(self, group):
        at = [which + i for which, piece in group for i in range(piece.shape[0] // LANES)]
        at = jnp.stack(at)
        distance = (at // self.blocks) ^ lax.axis_index("narrow")
        return jnp.stack([distance, at % self.blocks])

    def back(self, group, after, *shares, ahead=(), vmem_bytes=VMEM_BYTES):
        slots, width = self.normed.shape
        count, narrow = len(group), len(self.targets)
        features = sum(piece.shape[0] for _, piece in group)
        lanes = jax.ShapeDtypeStruct((slots, LANES), jnp.float32)
        blocks_ahead = sum(piece.shape[0] for _, piece in ahead) // LANES
        targets = [jax.ShapeDtypeStruct((slots, blocks_ahead * LANES), jnp.bfloat16)]
        targets = targets if ahead else []
        sizes = [share[0].shape[1] for share in shares]
        shared = [len(share) for share in shares]
        back, inner, *targets, token = local_kernel(
            functools.partial(
                back_body, count, shared, sizes, narrow, len(self.before) > 0, blocks_ahead
            ),
            [jax.ShapeDtypeStruct((slots, width), jnp.float32), lanes] + targets + [TOKEN],
            vmem_bytes=vmem_bytes,
            in_specs=[pl.BlockSpec(memory_space=pltpu.SMEM)]
            + anywhere(count)
            + in_vmem(sum(shared) + narrow + len(self.before))
            + in_hbm(1),
            out_specs=in_vmem(2 + len(targets)) + in_hbm(1),
            scratch_shapes=[
                pltpu.VMEM((slots, features), jnp.bfloat16),
                pltpu.VMEM((features, width), jnp.bfloat16),
                pltpu.SemaphoreType.DMA((count,)),
            ],
        )(
            self.places(group + list(ahead)),
            *[piece for _, piece in group],
            *[value for share in shares for value in share],
            *self.targets,
            *self.before,
            after,
        )
        self.before = (back, inner)
        self.last_target = targets
        return token

    def tail(self, group, shares):
        slots, width = self.normed.shape
        vocab_rows = self.place.shape[0]
        count = len(group)
        features = sum(piece.shape[0] for _, piece in group)
        return local_kernel(
            functools.partial(tail_body, count, self.width_all),
            jax.ShapeDtypeStruct((vocab_rows, width), jnp.bfloat16),
            vmem_bytes=END_VMEM_BYTES,
            in_specs=in_vmem(count + len(shares) + 7),
            out_specs=in_hbm(1)[0],
            scratch_shapes=[
                pltpu.VMEM((slots, features), jnp.bfloat16),
                pltpu.VMEM((width // COLUMNS, vocab_rows, COLUMNS), jnp.bfloat16),
                pltpu.VMEM((slots, COLUMNS), jnp.bfloat16),
                pltpu.SemaphoreType.DMA((width // COLUMNS,)),
            ],
        )(
            *[piece for _, piece in group],
            *shares,
            *self.last_target,
            *self.before,
            self.hidden,
            self.gain,
            self.scale,
            self.place,
        )


def plain_order(device, weight):
    device.ask()
    device.square(device.sent)
    device.pick(weight)
    device.share_targets()
    whole = lax.all_gather(weight, HOLDERS, axis=0, tiled=True)
    size = 4 * LANES
    groups = [
        [(jnp.int32(at // LANES), whole[at : at + size])] for at in range(0, whole.shape[0], size)
    ]
    token = weight
    for i, group in enumerate(groups[:-1]):
        projected, token = device.forward(group, token)
        ahead = groups[-1] if i == len(groups) - 2 else ()
        token = device.back(group, token, in_two_steps(projected), ahead=ahead)
    return device.tail(groups[-1], in_two_steps(device.forward(groups[-1], token)[0]))


def ring_order(device, weight):
    section, wide = lax.axis_index("section"), lax.axis_index("wide")
    holders = lax.axis_size(HOLDERS)
    at_ring = [i if i < holders // 2 else holders + holders // 2 - 1 - i for i in range(holders)]
    ring = jnp.where(section == 0, wide, holders - 1 - wide)

    def send(value, step):
        pairs = [(at_ring[i], at_ring[(i + step) % holders]) for i in range(holders)]
        return lax.ppermute(value, HOLDERS, pairs)

    def named(distance, piece, half=0):
        at = (ring + distance) % holders
        holder = jnp.where(at < holders // 2, at, holders + holders // 2 - 1 - at)
        return 2 * holder + half, piece

    up, down = send(weight, 1), send(weight, -1)
    device.ask()
    device.square(device.sent)

    (up, down), token = gate([up, down], device.arrived)
    near = [named(0, weight), named(-1, up), named(1, down)]
    up, down = send(up, 1), send(down, -1)
    device.pick(token)
    sum0, done = device.forward(near, token)
    shares0 = in_two_steps(sum0, 2)

    (up, down, device.target), token = gate([up, down, device.target], done)
    second = [named(-2, up), named(2, down)]
    up, down = send(up, 1), send(down, -1)
    device.share_targets()
    sum1, done = device.forward(second, token, END_VMEM_BYTES)
    shares1 = in_two_steps(sum1, 2)

    third = [named(-3, up), named(3, down)]
    up, down = send(up[:LANES], 1), send(down[LANES:], -1)
    sum2, done = device.forward(third, done, END_VMEM_BYTES)
    shares2 = in_two_steps(sum2, 2)
    done = device.back(near + second, done, shares0, shares1, vmem_bytes=END_VMEM_BYTES)

    last = [named(4, up), named(4, down, 1)]
    sum3, done = device.forward(last, done, END_VMEM_BYTES)
    shares3 = in_two_steps(sum3)
    device.back(third, done, shares2, ahead=last, vmem_bytes=END_VMEM_BYTES)
    return device.tail(last, shares3)


def on_device(token_shard, token_row, table, gain, key_value_weight, kv_target):
    device = Device(token_shard, token_row, table, gain, kv_target)
    holders = (lax.axis_size("section"), lax.axis_size("wide"))
    if holders == (2, 4) and key_value_weight.shape[0] == 2 * LANES:
        return ring_order(device, key_value_weight)
    return plain_order(device, key_value_weight)


def solution(mesh):
    return jax.shard_map(
        on_device,
        mesh=mesh,
        in_specs=(
            P(("section", "wide"), None),
            P(("section", "wide")),
            P(("section", "wide"), "narrow"),
            P("narrow"),
            P(("section", "wide"), "narrow"),
            P(("section", "wide"), "narrow"),
        ),
        out_specs=P(("section", "wide"), "narrow"),
        check_vma=False,
    )
```

```python
import functools

import jax
import jax.numpy as jnp
from jax import lax
from jax.experimental import pallas as pl
from jax.experimental.pallas import tpu as pltpu
from jax.sharding import PartitionSpec as P

EPSILON = 1e-05

HOLDERS = ("section", "wide")
LANES = 128
COLUMNS = 512
TAIL_COLUMNS = 1024
SMALL_COST = pl.CostEstimate(flops=1000, bytes_accessed=1000, transcendentals=0)


def contract_last(left, right):
    return lax.dot_general(
        left, right, (((1,), (1,)), ((), ())), preferred_element_type=jnp.float32
    )


def dot(left, right):
    return jnp.dot(left, right, preferred_element_type=jnp.float32)


VMEM_BYTES = 63 * 1024 * 1024
END_VMEM_BYTES = 18 * 1024 * 1024


def local_kernel(body, out_shape, vmem_bytes=VMEM_BYTES, **kwargs):
    return pl.pallas_call(
        body,
        out_shape=out_shape,
        compiler_params=pltpu.CompilerParams(vmem_limit_bytes=vmem_bytes),
        cost_estimate=SMALL_COST,
        **kwargs,
    )


def in_hbm(count):
    return [pl.BlockSpec(memory_space=pltpu.HBM)] * count


def anywhere(count):
    return [pl.BlockSpec(memory_space=pl.ANY)] * count


TOKEN = jax.ShapeDtypeStruct((8, LANES), jnp.float32)


def gate(values, *after):
    count = len(values)
    *values, token = local_kernel(
        lambda *refs: None,
        [jax.ShapeDtypeStruct(v.shape, v.dtype) for v in values] + [TOKEN],
        in_specs=anywhere(count + len(after)),
        out_specs=anywhere(count) + in_hbm(1),
        input_output_aliases={i: i for i in range(count)},
    )(*values, *after)
    return values, token


def in_vmem(count):
    return [pl.BlockSpec(memory_space=pltpu.VMEM)] * count


def slots_body(slot_count, shard_row, token_row, target, sent):
    tokens, width = target.shape
    slots = sent.shape[0]
    shard_here = shard_row[...]
    earlier = lax.broadcasted_iota(jnp.int32, (tokens, tokens), 0) < lax.broadcasted_iota(
        jnp.int32, (tokens, tokens), 1
    )
    shard_column = jnp.broadcast_to(shard_here.astype(jnp.float32), (tokens, tokens)).T
    same = (shard_column.astype(jnp.int32) == shard_here) & earlier
    rank = jnp.sum(jnp.where(same, 1.0, 0.0), axis=0, keepdims=True).astype(jnp.int32)
    position = shard_here * slot_count + rank
    here = lax.broadcasted_iota(jnp.int32, (slots, tokens), 0) == position
    to_slot = jnp.where(here, 1.0, 0.0)
    sent[:, :width] = dot(to_slot.astype(jnp.bfloat16), target[...]).astype(jnp.bfloat16)
    row = token_row[...]
    high = jnp.sum(to_slot * (row >> 8).astype(jnp.float32), axis=1, keepdims=True)
    low = jnp.sum(to_slot * (row & 255).astype(jnp.float32), axis=1, keepdims=True)
    taken = jnp.sum(to_slot, axis=1, keepdims=True)
    lane = lax.broadcasted_iota(jnp.int32, (slots, LANES), 1)
    numbers = jnp.where(
        lane == 0, high, jnp.where(lane == 1, low, jnp.where(lane == 2, taken, 0.0))
    )
    sent[:, width:] = numbers.astype(jnp.bfloat16)


def squares_body(table, _, squares, rows_buffer, copied):
    vocab_rows, width = table.shape
    count = copied.shape[0]
    per_copy = vocab_rows // count
    copies = []
    for i in range(count):
        rows = pl.ds(i * per_copy, per_copy)
        copies.append(pltpu.make_async_copy(table.at[rows], rows_buffer.at[rows], copied.at[i]))
        copies[-1].start()
    for i, copy in enumerate(copies):
        copy.wait()
        rows = slice(i * per_copy, (i + 1) * per_copy)
        total = jnp.zeros((per_copy, LANES), jnp.float32)
        for at in range(0, width, LANES):
            value = rows_buffer[rows, at : at + LANES].astype(jnp.float32)
            total += value * value
        total = jnp.broadcast_to(jnp.sum(total, axis=1, keepdims=True), total.shape)
        squares[:, rows] = total.T[: squares.shape[0]]


def pick_body(width_all, arrived, table, gain, *refs):
    shares, refs = refs[:-8], refs[-8:]
    _, hidden, normed, scale, target, place, rows_buffer, copied = refs
    vocab_rows, width = table.shape
    target_width = target.shape[0] * LANES
    blocks = [slice(at, at + COLUMNS) for at in range(0, width, COLUMNS)]
    copies = [
        pltpu.make_async_copy(table.at[:, block], rows_buffer.at[:, block], copied.at[i])
        for i, block in enumerate(blocks)
    ]
    for copy in copies:
        copy.start()
    here = arrived[...]
    slots = here.shape[0]
    numbers = here[:, target_width:].astype(jnp.float32)
    row = jnp.where(numbers[:, 2:3] > 0.5, numbers[:, 0:1] * 256.0 + numbers[:, 1:2], -1.0)
    picks = jnp.where(
        row.astype(jnp.int32) == lax.broadcasted_iota(jnp.int32, (slots, vocab_rows), 1), 1.0, 0.0
    )
    total = shares[0][:1]
    for share in shares[1:]:
        total += share[:1]
    row_scale = jnp.sum(picks * lax.rsqrt(total / width_all + EPSILON), axis=1, keepdims=True)
    scale[...] = jnp.broadcast_to(row_scale, scale.shape)
    place[...] = picks.T.astype(jnp.bfloat16)
    picks = picks.astype(jnp.bfloat16)
    for i in range(target.shape[0]):
        target[i] = here[:, i * LANES : (i + 1) * LANES]
    for copy, block in zip(copies, blocks):
        copy.wait()
        rows = dot(picks, rows_buffer[:, block])
        hidden[:, block] = rows.astype(jnp.bfloat16)
        normed[:, block] = (rows * row_scale * gain[:, block]).astype(jnp.bfloat16)


def start_pieces(pieces, buffer, copied):
    copies, first = [], 0
    for i, piece in enumerate(pieces):
        rows = pl.ds(first, piece.shape[0])
        copies.append(pltpu.make_async_copy(piece, buffer.at[rows], copied.at[i]))
        copies[-1].start()
        first += piece.shape[0]
    return copies


def forward_body(count, normed, *refs):
    pieces, refs = refs[:count], refs[count:]
    _, out, _, rows_buffer, buffer, copied = refs
    rows = pltpu.make_async_copy(normed, rows_buffer, copied.at[count])
    rows.start()
    copies = start_pieces(pieces, buffer, copied)
    rows.wait()
    first = last = 0
    for piece, copy in zip(pieces, copies):
        copy.wait()
        last += piece.shape[0]
        if last - first >= 2 * LANES or last == buffer.shape[0]:
            part = slice(first, last)
            out[:, part] = contract_last(rows_buffer[...], buffer[part]).astype(out.dtype)
            first = last


def target_at(places, i, targets):
    distance, block = places[0, i], places[1, i]
    value = targets[0][block]
    for d in range(1, len(targets)):
        value = jnp.where(distance == d, targets[d][block], value)
    return value.astype(jnp.float32)


def residual_of(places, shares, targets, inner, residual, first=0, last=None):
    last = residual.shape[1] // LANES if last is None else last
    for i in range(first, last):
        lanes = slice((i - first) * LANES, (i - first + 1) * LANES)
        value = shares[0][:, lanes].astype(jnp.float32)
        for share in shares[1:]:
            value += share[:, lanes].astype(jnp.float32)
        rounded = (value - target_at(places, i, targets)).astype(jnp.bfloat16)
        residual[:, i * LANES : (i + 1) * LANES] = rounded
        inner = inner + rounded.astype(jnp.float32) * value
    return inner


def back_body(count, shared, features, narrow, before, ahead, places, *refs):
    pieces, refs = refs[:count], refs[count:]
    shares = []
    for size in shared:
        shares.append(refs[:size])
        refs = refs[size:]
    targets, refs = refs[:narrow], refs[narrow:]
    if before:
        back_in, inner_in, refs = refs[0], refs[1], refs[2:]
    _, back_out, inner_out, *target_out, _, residual, buffer, copied = refs
    copies = start_pieces(pieces, buffer, copied)
    inner = inner_in[...] if before else jnp.zeros(inner_out.shape, jnp.float32)
    first = 0
    for group, size in zip(shares, features):
        last = first + size // LANES
        inner = residual_of(places, group, targets, inner, residual, first, last)
        first = last
    inner_out[...] = inner
    for i in range(ahead):
        lanes = slice(i * LANES, (i + 1) * LANES)
        target_out[0][:, lanes] = target_at(places, first + i, targets).astype(jnp.bfloat16)
    for copy in copies:
        copy.wait()
    for at in range(0, back_out.shape[1], COLUMNS):
        part = slice(at, at + COLUMNS)
        value = dot(residual[...], buffer[:, part])
        back_out[:, part] = value + back_in[:, part] if before else value


def tail_body(count, width, *refs):
    pieces, refs = refs[:count], refs[count:]
    shares, refs = refs[:-12], refs[-12:]
    target, back_in, inner_in, hidden, gain, scale, place, table_grad, *refs = refs
    residual, buffer, row_grad, copied = refs
    inner = inner_in[...]
    for at in range(0, residual.shape[1], LANES):
        lanes = slice(at, at + LANES)
        value = shares[0][:, lanes].astype(jnp.float32)
        for share in shares[1:]:
            value += share[:, lanes].astype(jnp.float32)
        rounded = (value - target[:, lanes].astype(jnp.float32)).astype(jnp.bfloat16)
        residual[:, lanes] = rounded
        inner += rounded.astype(jnp.float32) * value
    row_scale = scale[:, :1]
    factor = row_scale * row_scale * (jnp.sum(inner, axis=1, keepdims=True) / width)
    copies = []
    size = buffer.shape[2]
    for i in range(copied.shape[0]):
        block = slice(i * size, (i + 1) * size)
        back = back_in[:, block]
        weights = jnp.concatenate([piece[:, block] for piece in pieces], axis=0)
        back += dot(residual[...], weights)
        row_grad[...] = (
            row_scale * (back * gain[:, block]) - hidden[:, block].astype(jnp.float32) * factor
        ).astype(jnp.bfloat16)
        buffer[i] = dot(place[...], row_grad[...]).astype(jnp.bfloat16)
        copies.append(pltpu.make_async_copy(buffer.at[i], table_grad.at[:, block], copied.at[i]))
        copies[-1].start()
    for copy in copies:
        copy.wait()


def exchange_narrow(value, distance):
    narrow = lax.axis_size("narrow")
    return lax.ppermute(value, "narrow", [(i, i ^ distance) for i in range(narrow)])


def in_one_step(value):
    return [value] + [exchange_narrow(value, d) for d in range(1, lax.axis_size("narrow"))]


def in_two_steps(value, first=1):
    half = value.astype(jnp.float32) + exchange_narrow(value, first).astype(jnp.float32)
    half = half.astype(jnp.bfloat16)
    return [half, exchange_narrow(half, 3 - first)]


class Device:
    def __init__(self, token_shard, token_row, table, gain, kv_target):
        self.tokens = (token_shard, token_row, kv_target)
        self.table = table
        self.gain = gain.reshape(1, table.shape[1])
        self.owners = lax.axis_size(HOLDERS)
        self.slot_count = 2 * kv_target.shape[0] // self.owners
        self.slots = self.owners * self.slot_count
        self.blocks = kv_target.shape[1] // LANES
        self.width_all = table.shape[1] * lax.axis_size("narrow")
        self.before = ()

    def ask(self):
        token_shard, token_row, target = self.tokens
        tokens, width = target.shape
        self.sent = local_kernel(
            functools.partial(slots_body, self.slot_count),
            jax.ShapeDtypeStruct((self.slots, width + LANES), jnp.bfloat16),
        )(token_shard.reshape(1, tokens), token_row.reshape(1, tokens), target)
        self.arrived = lax.all_to_all(
            self.sent.reshape(self.owners, self.slot_count, width + LANES),
            HOLDERS,
            split_axis=0,
            concat_axis=0,
            tiled=True,
        ).reshape(self.slots, width + LANES)

    def square(self, after):
        vocab_rows, width = self.table.shape
        squares = local_kernel(
            squares_body,
            jax.ShapeDtypeStruct((8, vocab_rows), jnp.float32),
            in_specs=in_hbm(2),
            scratch_shapes=[
                pltpu.VMEM((vocab_rows, width), jnp.bfloat16),
                pltpu.SemaphoreType.DMA((vocab_rows // LANES,)),
            ],
        )(self.table, after)
        self.squares = in_one_step(squares)

    def pick(self, after):
        vocab_rows, width = self.table.shape
        rows = jax.ShapeDtypeStruct((self.slots, width), jnp.bfloat16)
        self.hidden, self.normed, self.scale, self.target, self.place = local_kernel(
            functools.partial(pick_body, self.width_all),
            (
                rows,
                rows,
                jax.ShapeDtypeStruct((self.slots, LANES), jnp.float32),
                jax.ShapeDtypeStruct((self.blocks, self.slots, LANES), jnp.bfloat16),
                jax.ShapeDtypeStruct((vocab_rows, self.slots), jnp.bfloat16),
            ),
            in_specs=in_vmem(1) + in_hbm(1) + in_vmem(1 + len(self.squares)) + in_hbm(1),
            scratch_shapes=[
                pltpu.VMEM((vocab_rows, width), jnp.bfloat16),
                pltpu.SemaphoreType.DMA((width // COLUMNS,)),
            ],
        )(self.arrived, self.table, self.gain, *self.squares, after)

    def share_targets(self):
        along = exchange_narrow(self.target, 2)
        across = exchange_narrow(self.target, 1)
        self.targets = [self.target, across, along, exchange_narrow(along, 1)]

    def forward(self, group, after, vmem_bytes=VMEM_BYTES):
        count = len(group)
        features = sum(piece.shape[0] for _, piece in group)
        slots, width = self.normed.shape
        return local_kernel(
            functools.partial(forward_body, count),
            (jax.ShapeDtypeStruct((slots, features), jnp.bfloat16), TOKEN),
            vmem_bytes=vmem_bytes,
            in_specs=in_hbm(1) + anywhere(count) + in_hbm(1),
            out_specs=in_vmem(1) + in_hbm(1),
            scratch_shapes=[
                pltpu.VMEM((slots, width), jnp.bfloat16),
                pltpu.VMEM((features, width), jnp.bfloat16),
                pltpu.SemaphoreType.DMA((count + 1,)),
            ],
        )(self.normed, *[piece for _, piece in group], after)

    def places(self, group):
        at = [which + i for which, piece in group for i in range(piece.shape[0] // LANES)]
        at = jnp.stack(at)
        distance = (at // self.blocks) ^ lax.axis_index("narrow")
        return jnp.stack([distance, at % self.blocks])

    def back(self, group, after, *shares, ahead=(), vmem_bytes=VMEM_BYTES):
        slots, width = self.normed.shape
        count, narrow = len(group), len(self.targets)
        features = sum(piece.shape[0] for _, piece in group)
        lanes = jax.ShapeDtypeStruct((slots, LANES), jnp.float32)
        blocks_ahead = sum(piece.shape[0] for _, piece in ahead) // LANES
        targets = [jax.ShapeDtypeStruct((slots, blocks_ahead * LANES), jnp.bfloat16)]
        targets = targets if ahead else []
        sizes = [share[0].shape[1] for share in shares]
        shared = [len(share) for share in shares]
        back, inner, *targets, token = local_kernel(
            functools.partial(
                back_body, count, shared, sizes, narrow, len(self.before) > 0, blocks_ahead
            ),
            [jax.ShapeDtypeStruct((slots, width), jnp.float32), lanes] + targets + [TOKEN],
            vmem_bytes=vmem_bytes,
            in_specs=[pl.BlockSpec(memory_space=pltpu.SMEM)]
            + anywhere(count)
            + in_vmem(sum(shared) + narrow + len(self.before))
            + in_hbm(1),
            out_specs=in_vmem(2 + len(targets)) + in_hbm(1),
            scratch_shapes=[
                pltpu.VMEM((slots, features), jnp.bfloat16),
                pltpu.VMEM((features, width), jnp.bfloat16),
                pltpu.SemaphoreType.DMA((count,)),
            ],
        )(
            self.places(group + list(ahead)),
            *[piece for _, piece in group],
            *[value for share in shares for value in share],
            *self.targets,
            *self.before,
            after,
        )
        self.before = (back, inner)
        self.last_target = targets
        return token

    def tail(self, group, shares):
        slots, width = self.normed.shape
        vocab_rows = self.place.shape[0]
        count = len(group)
        features = sum(piece.shape[0] for _, piece in group)
        return local_kernel(
            functools.partial(tail_body, count, self.width_all),
            jax.ShapeDtypeStruct((vocab_rows, width), jnp.bfloat16),
            vmem_bytes=END_VMEM_BYTES,
            in_specs=in_vmem(count + len(shares) + 7),
            out_specs=in_hbm(1)[0],
            scratch_shapes=[
                pltpu.VMEM((slots, features), jnp.bfloat16),
                pltpu.VMEM((width // TAIL_COLUMNS, vocab_rows, TAIL_COLUMNS), jnp.bfloat16),
                pltpu.VMEM((slots, TAIL_COLUMNS), jnp.bfloat16),
                pltpu.SemaphoreType.DMA((width // TAIL_COLUMNS,)),
            ],
        )(
            *[piece for _, piece in group],
            *shares,
            *self.last_target,
            *self.before,
            self.hidden,
            self.gain,
            self.scale,
            self.place,
        )


def plain_order(device, weight):
    device.ask()
    device.square(device.sent)
    device.pick(weight)
    device.share_targets()
    whole = lax.all_gather(weight, HOLDERS, axis=0, tiled=True)
    size = 4 * LANES
    groups = [
        [(jnp.int32(at // LANES), whole[at : at + size])] for at in range(0, whole.shape[0], size)
    ]
    token = weight
    for i, group in enumerate(groups[:-1]):
        projected, token = device.forward(group, token)
        ahead = groups[-1] if i == len(groups) - 2 else ()
        token = device.back(group, token, in_two_steps(projected), ahead=ahead)
    return device.tail(groups[-1], in_two_steps(device.forward(groups[-1], token)[0]))


def ring_order(device, weight):
    section, wide = lax.axis_index("section"), lax.axis_index("wide")
    holders = lax.axis_size(HOLDERS)
    at_ring = [i if i < holders // 2 else holders + holders // 2 - 1 - i for i in range(holders)]
    ring = jnp.where(section == 0, wide, holders - 1 - wide)

    def send(value, step):
        pairs = [(at_ring[i], at_ring[(i + step) % holders]) for i in range(holders)]
        return lax.ppermute(value, HOLDERS, pairs)

    def named(distance, piece, half=0):
        at = (ring + distance) % holders
        holder = jnp.where(at < holders // 2, at, holders + holders // 2 - 1 - at)
        return 2 * holder + half, piece

    up, down = send(weight, 1), send(weight, -1)
    device.ask()
    device.square(device.sent)

    (up, down), token = gate([up, down], device.arrived)
    near = [named(0, weight), named(-1, up), named(1, down)]
    up, down = send(up, 1), send(down, -1)
    device.pick(token)
    sum0, done = device.forward(near, token)
    shares0 = in_two_steps(sum0, 2)

    (up, down, device.target), token = gate([up, down, device.target], done)
    second = [named(-2, up), named(2, down)]
    up, down = send(up, 1), send(down, -1)
    device.share_targets()
    sum1, done = device.forward(second, token, END_VMEM_BYTES)
    shares1 = in_two_steps(sum1, 2)

    third = [named(-3, up), named(3, down)]
    up, down = send(up[:LANES], 1), send(down[LANES:], -1)
    sum2, done = device.forward(third, done, END_VMEM_BYTES)
    shares2 = in_two_steps(sum2, 2)
    done = device.back(near + second, done, shares0, shares1, vmem_bytes=END_VMEM_BYTES)

    last = [named(4, up), named(4, down, 1)]
    sum3, done = device.forward(last, done, END_VMEM_BYTES)
    shares3 = in_two_steps(sum3)
    device.back(third, done, shares2, ahead=last, vmem_bytes=END_VMEM_BYTES)
    return device.tail(last, shares3)


def on_device(token_shard, token_row, table, gain, key_value_weight, kv_target):
    device = Device(token_shard, token_row, table, gain, kv_target)
    holders = (lax.axis_size("section"), lax.axis_size("wide"))
    if holders == (2, 4) and key_value_weight.shape[0] == 2 * LANES:
        return ring_order(device, key_value_weight)
    return plain_order(device, key_value_weight)


def solution(mesh):
    return jax.shard_map(
        on_device,
        mesh=mesh,
        in_specs=(
            P(("section", "wide"), None),
            P(("section", "wide")),
            P(("section", "wide"), "narrow"),
            P("narrow"),
            P(("section", "wide"), "narrow"),
            P(("section", "wide"), "narrow"),
        ),
        out_specs=P(("section", "wide"), "narrow"),
        check_vma=False,
    )
```
